32 devices in a mesh: plane: 4 (over y, x), tile: 8 (over z, core).
Axes of the slice: x: 2, y: 2, z: 4, core: 2. Of those that a mesh axis runs over, the one named last changes fastest.
Arguments:
- density: float32 [12, 64, 2048], P('plane', 'tile'), may hold values from -6 to 6
- plane_slot: int32 [12], replicated, may hold values from 0 to 23, as said below
- paint_weight: float32 [32, 9], replicated, may hold values from -2 to 2
- paint_bias: float32 [32], replicated, may hold values from -0.5 to 0.5
- mix_weight: float32 [32], replicated, may hold values from -1 to 1
- short_kernel: float32 [5, 5], replicated, may hold values from -1 to 1
Outputs:
- distortion: float32 [4, 12, 64, 2048], P(None, 'plane', 'tile')
The draws below stay inside these ranges and needn't reach their ends.
Inputs may be any that keep to these rules, and one draw needn't show every extreme that they name: `plane_slot`: strictly increasing along the planes; the first is 0 and the last is 23.
All inputs are finite; a program needn't handle non-finite values.
Results may differ from the reference program's by a relative error of at most 0.00026.
Values sent between devices are 32-bit elements; how exact they have to be, the bound alone decides.
A program may use at most 64 MiB of HBM per device.

```python
import math
import jax
import jax.numpy as jnp
from jax import lax

TR = 8
NC = 2048
CH = 32
NPL = 12
NR = 64
SLOTS = 24
N_TILE = 8


def draw_density(key, part):
    values = jnp.clip(jax.random.normal(key, (NPL, NR, NC), jnp.float32), -6.0, 6.0)
    return values


def draw_plane_slot(key, part):
    inner = 1 + jax.random.permutation(key, SLOTS - 2)[:NPL - 2]
    chosen = jnp.concatenate([jnp.zeros((1,), jnp.int32), inner.astype(jnp.int32), jnp.full((1,), SLOTS - 1, jnp.int32)])
    return jnp.sort(chosen)


def scatter_about(rng, extent, deviation, bound, kind=jnp.bfloat16):
    return jnp.clip(deviation * jax.random.normal(rng, extent, jnp.float32), -bound, bound).astype(kind)


def setup_inputs(seed: int = 0) -> dict:
    arg_keys = jax.random.split(jax.random.key(seed), 7)
    return {
        "density": draw_density(jax.random.fold_in(arg_keys[6], 71), 0),
        "plane_slot": draw_plane_slot(jax.random.fold_in(arg_keys[6], 71), 0),
        "paint_weight": scatter_about(arg_keys[2], (CH, 9), 9 ** -0.5, 2.0, jnp.float32),
        "paint_bias": jnp.clip(jax.random.uniform(arg_keys[3], (CH,), jnp.float32, -0.5, 0.5), -0.5, 0.5),
        "mix_weight": scatter_about(arg_keys[4], (CH,), CH ** -0.5, 1.0, jnp.float32),
        "short_kernel": scatter_about(arg_keys[5], (5, 5), 0.2, 1.0, jnp.float32),
    }


highest = lax.Precision.HIGHEST
lens_gain = 0.25

def paint_rows(extended, paint_weight, paint_bias, mix_weight):
    row_count = extended.shape[-2] - 4
    col_count = extended.shape[-1]
    padded = jnp.pad(extended, [(0, 0)] * (extended.ndim - 1) + [(2, 2)])
    stacked = jnp.stack([padded[..., 2 + 2 * row_step:2 + 2 * row_step + row_count, 2 + 2 * col_step:2 + 2 * col_step + col_count] for row_step in (-1, 0, 1) for col_step in (-1, 0, 1)], axis=0)
    before = jnp.einsum('ct,t...->c...', paint_weight, stacked, precision=highest)
    hidden = jnp.tanh(before + paint_bias.reshape((-1,) + (1,) * (before.ndim - 1)))
    return jnp.einsum('c,c...->...', mix_weight, hidden, precision=highest)

def short_rows(extended, short_kernel):
    row_count = extended.shape[-2] - 4
    col_count = extended.shape[-1]
    padded = jnp.pad(extended, [(0, 0)] * (extended.ndim - 1) + [(2, 2)])
    running = jnp.zeros(extended.shape[:-2] + (row_count, col_count), jnp.float32)
    for row_tap in range(5):
        for col_tap in range(5):
            running = running + short_kernel[row_tap, col_tap] * padded[..., row_tap:row_tap + row_count, col_tap:col_tap + col_count]
    return running

def hessian_rows(extended):
    padded = jnp.pad(extended, [(0, 0)] * (extended.ndim - 1) + [(1, 1)])
    center = padded[..., 1:-1, 1:-1]
    second_rows = padded[..., 2:, 1:-1] - 2.0 * center + padded[..., :-2, 1:-1]
    second_cols = padded[..., 1:-1, 2:] - 2.0 * center + padded[..., 1:-1, :-2]
    mixed_part = (padded[..., 2:, 2:] - padded[..., 2:, :-2] - padded[..., :-2, 2:] + padded[..., :-2, :-2]) * 0.25
    return jnp.stack([second_rows, second_cols, mixed_part], axis=0)

def lens_step(lens_state, shear_field, mixing, bending):
    previous = lens_state[0:2]
    current = lens_state[2:4]
    bent_first = shear_field[0] * current[0] + shear_field[2] * current[1]
    bent_second = shear_field[2] * current[0] + shear_field[1] * current[1]
    bent_rows = jnp.stack([bent_first, bent_second], axis=0)
    advanced = (1.0 - mixing) * previous + mixing * current - bending * bent_rows
    return jnp.concatenate([current, advanced], axis=0)

def distances(plane_slot, slot_total):
    distance = (plane_slot.astype(jnp.float32) + 1.0) / slot_total
    before = jnp.concatenate([jnp.zeros((1,), jnp.float32), distance[:-1]])
    after = jnp.concatenate([distance[1:], jnp.full((1,), (slot_total + 1.0) / slot_total, jnp.float32)])
    mixing = before * (after - distance) / (distance * (after - before))
    bending = lens_gain * (after - distance) / after
    return (mixing, bending)

def coarse_kernel(row_global, col_global, scale):
    gap = row_global.astype(jnp.float32)[:, None] - col_global.astype(jnp.float32)[None, :]
    return jnp.exp(-jnp.abs(gap) / scale)

def reference(density, plane_slot, paint_weight, paint_bias, mix_weight, short_kernel):
    total_rows = TR * N_TILE
    coarse_rows = total_rows // 4
    coarse_cols = NC // 4
    row_scale = total_rows / 16.0
    col_scale = NC / 16.0
    long_gain = 1.0 / math.sqrt(row_scale * col_scale)
    row_kernel = coarse_kernel(jnp.arange(coarse_rows, dtype=jnp.int32), jnp.arange(coarse_rows, dtype=jnp.int32), row_scale)
    col_kernel = coarse_kernel(jnp.arange(coarse_cols, dtype=jnp.int32), jnp.arange(coarse_cols, dtype=jnp.int32), col_scale)
    mixing, bending = distances(plane_slot, SLOTS)

    def one_plane(lens_state, inputs):
        plane_map, mixing_here, bending_here = inputs
        convergence = paint_rows(jnp.pad(plane_map, ((2, 2), (0, 0))), paint_weight, paint_bias, mix_weight)
        short_part = short_rows(jnp.pad(convergence, ((2, 2), (0, 0))), short_kernel)
        coarse = convergence.reshape(coarse_rows, 4, coarse_cols, 4).mean(axis=(1, 3))
        long_part = long_gain * jnp.dot(jnp.dot(row_kernel, coarse, precision=highest), col_kernel, precision=highest)
        potential = short_part + jnp.repeat(jnp.repeat(long_part, 4, axis=0), 4, axis=1)
        shear_field = hessian_rows(jnp.pad(potential, ((1, 1), (0, 0))))
        lens_state = lens_step(lens_state, shear_field, mixing_here, bending_here)
        return (lens_state, lens_state[2:4].reshape(4, total_rows, NC))
    pattern = jnp.array([[1.0, 0.0], [0.0, 1.0], [1.0, 0.0], [0.0, 1.0]], jnp.float32)
    start_state = jnp.broadcast_to(pattern[:, :, None, None], (4, 2, total_rows, NC)).astype(jnp.float32)
    unused_state, results = lax.scan(one_plane, start_state, (density, mixing, bending))
    return jnp.transpose(results, (1, 0, 2, 3))
```

```python
import functools
import math

import jax
import jax.numpy as jnp
from jax import lax
from jax.experimental import pallas as pl
from jax.experimental.pallas import tpu as pltpu
from jax.sharding import PartitionSpec as P

lens_gain = 0.25
pad = 128
block = 512
f32 = jnp.float32
bf16 = jnp.bfloat16


def split(x):
    hi = x.astype(bf16)
    return hi, (x - hi.astype(f32)).astype(bf16)


def iota(shape, axis):
    return lax.broadcasted_iota(jnp.int32, shape, axis)


def dot(a, b):
    return jnp.dot(a, b, preferred_element_type=f32)


def kernel(
    tiles, groups, density, slot, weight, bias, mix, short, out,
    ext, conv, paint_lhs, short_lhs, col_hi, col_lo, spread, gathered, shorts, longs,
    halo_send, halo_recv, coarse_send, coarse_recv, short_send, short_recv, long_send, long_recv,
):
    planes, rows, cols = density.shape
    channels = weight.shape[0]
    slots = slot.shape[0]
    coarse_cols = cols // 4
    t = lax.axis_index("tile")
    g = lax.axis_index("plane")

    barrier = pltpu.get_barrier_semaphore()

    def greet_tile(j, carry):
        pl.semaphore_signal(barrier, inc=1, device_id={"tile": lax.rem(t + j, tiles)})
        return carry

    def greet_plane(j, carry):
        pl.semaphore_signal(barrier, inc=1, device_id={"plane": lax.rem(g + j, groups)})
        return carry

    lax.fori_loop(1, tiles, greet_tile, 0)
    lax.fori_loop(1, groups, greet_plane, 0)
    pl.semaphore_wait(barrier, tiles + groups - 2)

    def halo_copy(side):
        return pltpu.make_async_remote_copy(
            src_ref=density,
            dst_ref=ext.at[2 * side, :, :, pl.ds(pad, cols)],
            send_sem=halo_send.at[side],
            recv_sem=halo_recv.at[side],
            device_id={"tile": lax.rem(t + (1 if side == 0 else tiles - 1), tiles)},
        )

    has_low = t > 0
    has_high = t < tiles - 1

    @pl.when(has_high)
    def _():
        halo_copy(0).start()

    @pl.when(has_low)
    def _():
        halo_copy(1).start()

    ext[:, :, :, 0:pad] = jnp.zeros((3, planes, rows, pad), f32)
    ext[:, :, :, pad + cols :] = jnp.zeros((3, planes, rows, pad), f32)
    ext[1, :, :, pad : pad + cols] = density[...]
    conv[:, :, 0:pad] = jnp.zeros((planes, 16, pad), f32)
    conv[:, :, pad + cols :] = jnp.zeros((planes, 16, pad), f32)

    @pl.when(jnp.logical_not(has_low))
    def _():
        ext[0, :, :, pad : pad + cols] = jnp.zeros((planes, rows, cols), f32)

    @pl.when(jnp.logical_not(has_high))
    def _():
        ext[2, :, :, pad : pad + cols] = jnp.zeros((planes, rows, cols), f32)

    lane = iota((16, 240), 1)
    sub = iota((16, 240), 0)
    seg = jnp.where(lane >= 160, lane - 160, jnp.where(lane >= 80, lane - 80, lane))
    tap_masks = []
    for i in range(3):
        for j in range(3):
            tap_masks.append(seg == j * 24 + sub + 4 + 2 * (i - 1))

    def pack(value):
        hi = value.astype(bf16).astype(f32)
        return jnp.where(lane < 160, hi, value - hi).astype(bf16)

    def paint_channel(c, carry):
        value = jnp.zeros((16, 240), f32)
        for tap in range(9):
            value = jnp.where(tap_masks[tap], weight[c, tap], value)
        paint_lhs[pl.ds(pl.multiple_of(c * 16, 16), 16), :] = pack(value)
        return carry

    lax.fori_loop(0, channels, paint_channel, 0)

    row_of = jnp.where(sub < 8, sub, jnp.where(sub == 8, -1, 8))
    value = jnp.zeros((16, 240), f32)
    for a in range(5):
        for b in range(5):
            value = jnp.where(
                (seg == b * 16 + row_of + 2 + a) & (sub < 10), short[a, b], value
            )
    short_lhs[...] = pack(value)

    spread[...] = ((iota((128, block), 1) >> 2) == iota((128, block), 0)).astype(f32).astype(bf16)
    pool = ((iota((block, 128), 0) >> 2) == iota((block, 128), 1)).astype(f32).astype(bf16)
    col_scale = cols / 16.0

    def col_rows(i, carry):
        gap = iota((64, coarse_cols), 0) + i * 64 - iota((64, coarse_cols), 1)
        hi, lo = split(jnp.exp(-jnp.abs(gap.astype(f32)) / col_scale))
        at = pl.ds(pl.multiple_of(i * 64, 64), 64)
        col_hi[at, :] = hi
        col_lo[at, :] = lo
        return carry

    lax.fori_loop(0, coarse_cols // 64, col_rows, 0)

    @pl.when(has_low)
    def _():
        halo_copy(0).wait_recv()

    @pl.when(has_high)
    def _():
        halo_copy(1).wait_recv()

    row_global = iota((16, block), 0) + (t * rows - 4)
    row_real = (row_global >= 0) & (row_global < tiles * rows)

    def paint(cb, carry):
        window = pl.ds(pl.multiple_of(cb * block, block), block + 2 * pad)
        sums = []
        for p in range(planes):
            parts = [ext[s, p, :, window] for s in range(3)]
            stacked = []
            for j in range(3):
                start = pad + 2 * (j - 1)
                stacked += [part[:, start : start + block] for part in parts]
            stacked.append(jnp.zeros((8, block), f32))
            hi, lo = split(jnp.concatenate(stacked, axis=0))
            pre = dot(paint_lhs[...], jnp.concatenate([hi, lo, hi], axis=0))
            total = jnp.zeros((16, block), f32)
            for c in range(channels):
                total += mix[c] * jnp.tanh(pre[16 * c : 16 * c + 16] + bias[c])
            total = jnp.where(row_real, total, 0.0)
            conv[p, :, pl.ds(pl.multiple_of(cb * block + pad, pad), block)] = total
            sums.append(jnp.sum(total[4:8], axis=0, keepdims=True))
            sums.append(jnp.sum(total[8:12], axis=0, keepdims=True))
        sums += [jnp.zeros((1, block), f32)] * (8 - 2 * planes)
        hi, lo = split(jnp.concatenate(sums, axis=0) * (1.0 / 16.0))
        coarse = dot(hi, pool) + dot(lo, pool)
        gathered[t, :, pl.ds(pl.multiple_of(cb * 128, 128), 128)] = coarse
        return carry

    lax.fori_loop(0, cols // block, paint, 0)

    def coarse_copy(j):
        return pltpu.make_async_remote_copy(
            src_ref=gathered.at[t],
            dst_ref=gathered.at[t],
            send_sem=coarse_send.at[j],
            recv_sem=coarse_recv.at[t],
            device_id={"tile": lax.rem(t + j, tiles)},
        )

    def coarse_start(j, carry):
        coarse_copy(j).start()
        return carry

    lax.fori_loop(1, tiles, coarse_start, 0)

    def short_block(cb, carry):
        window = pl.ds(pl.multiple_of(cb * block, block), block + 2 * pad)
        at = pl.ds(pl.multiple_of(cb * block, block), block)
        edges = []
        for p in range(planes):
            part = conv[p, :, window]
            stacked = [part[:, pad + b - 2 : pad + b - 2 + block] for b in range(5)]
            hi, lo = split(jnp.concatenate(stacked, axis=0))
            value = dot(short_lhs[...], jnp.concatenate([hi, lo, hi], axis=0))
            shorts[g, p, :, at] = value[0:8]
            edges.append(value[8:10])
        edges += [jnp.zeros((8 - 2 * planes, block), f32)]
        shorts[g, planes, :, at] = jnp.concatenate(edges, axis=0)
        return carry

    lax.fori_loop(0, cols // block, short_block, 0)

    def later_copy(buffer, send, recv, to):
        return pltpu.make_async_remote_copy(
            src_ref=buffer.at[g],
            dst_ref=buffer.at[g],
            send_sem=send.at[to],
            recv_sem=recv.at[g],
            device_id={"plane": to},
        )

    def short_start(to, carry):
        later_copy(shorts, short_send, short_recv, to).start()
        return carry

    lax.fori_loop(g + 1, groups, short_start, 0)

    def coarse_wait(j, carry):
        source = lax.rem(t + j, tiles)
        pltpu.make_async_remote_copy(
            src_ref=gathered.at[source],
            dst_ref=gathered.at[source],
            send_sem=coarse_send.at[j],
            recv_sem=coarse_recv.at[source],
            device_id={"tile": source},
        ).wait_recv()
        return carry

    lax.fori_loop(1, tiles, coarse_wait, 0)
    row_scale = tiles * rows / 16.0
    long_gain = 1.0 / math.sqrt(row_scale * col_scale)
    m = iota((16, tiles * 8), 0)
    n = iota((16, tiles * 8), 1)
    gap = (2 * t - 1 + (m & 3)) - (2 * (n >> 3) + (n & 1))
    near = jnp.exp(-jnp.abs(gap.astype(f32)) / row_scale) * long_gain
    row_kernel = jnp.where((m >> 2) == ((n & 7) >> 1), near, 0.0)
    everything = gathered[...].reshape(tiles * 8, coarse_cols)
    summed = jnp.dot(
        row_kernel, everything, preferred_element_type=f32, precision=lax.Precision.HIGHEST
    )
    hi, lo = split(summed)
    longs[g] = dot(hi, col_hi[...]) + dot(lo, col_hi[...]) + dot(hi, col_lo[...])

    def long_start(to, carry):
        later_copy(longs, long_send, long_recv, to).start()
        return carry

    lax.fori_loop(g + 1, groups, long_start, 0)

    for entry in range(4):
        for p in (planes - 2, planes - 1):
            out[entry, p] = jnp.full((rows, cols), 1.0 if entry in (0, 3) else 0.0, f32)
    row_at = iota((rows, cols), 0)
    col_at = iota((rows, cols), 1)
    low_gain = jnp.where(t > 0, 1.0, 0.0)
    high_gain = jnp.where(t < tiles - 1, 1.0, 0.0)
    slot_total = 2.0 * slots
    wide = cols // 128

    def next_col(x):
        return jnp.where(col_at == cols - 1, 0.0, pltpu.roll(x, cols - 1, 1))

    def last_col(x):
        return jnp.where(col_at == 0, 0.0, pltpu.roll(x, 1, 1))

    def lens(gi, carry):
        @pl.when(gi < g)
        def _():
            for buffer, send, recv in (
                (shorts, short_send, short_recv), (longs, long_send, long_recv)
            ):
                pltpu.make_async_remote_copy(
                    src_ref=buffer.at[gi],
                    dst_ref=buffer.at[gi],
                    send_sem=send.at[gi],
                    recv_sem=recv.at[gi],
                    device_id={"plane": gi},
                ).wait_recv()

        hi, lo = split(longs[gi])
        pieces = coarse_cols // 128
        stacked = [x[:, 128 * b : 128 * b + 128] for x in (hi, lo) for b in range(pieces)]
        spread_out = dot(jnp.concatenate(stacked, axis=0), spread[...])
        upper = [
            spread_out[16 * b : 16 * b + 16]
            + spread_out[16 * (pieces + b) : 16 * (pieces + b) + 16]
            for b in range(pieces)
        ]
        long_wide = jnp.concatenate(upper, axis=1)
        edges = shorts[gi, planes]
        for p in range(planes):
            k = gi * planes + p

            def distance(index):
                value = jnp.full((8, 128), slot[index], jnp.int32)
                return (value.astype(f32) + 1.0) / slot_total

            here = distance(k)
            before = jnp.where(k > 0, distance(jnp.maximum(k - 1, 0)), 0.0)
            after = jnp.where(
                k < slots - 1,
                distance(jnp.minimum(k + 1, slots - 1)),
                (slot_total + 1.0) / slot_total,
            )
            mixing = before * (after - here) / (here * (after - before))
            bending = lens_gain * (after - here) / after
            mixing = jnp.concatenate([mixing] * wide, axis=1)
            bending = jnp.concatenate([bending] * wide, axis=1)
            center = shorts[gi, p] + jnp.where(
                row_at < 4, long_wide[4 * p + 1 : 4 * p + 2], long_wide[4 * p + 2 : 4 * p + 3]
            )
            top = (edges[2 * p : 2 * p + 1] + long_wide[4 * p : 4 * p + 1]) * low_gain
            bottom = (
                edges[2 * p + 1 : 2 * p + 2] + long_wide[4 * p + 3 : 4 * p + 4]
            ) * high_gain
            up = jnp.where(row_at == 0, top, pltpu.roll(center, 1, 0))
            down = jnp.where(row_at == rows - 1, bottom, pltpu.roll(center, rows - 1, 0))
            u11 = (down - 2.0 * center + up) * bending
            u22 = (next_col(center) - 2.0 * center + last_col(center)) * bending
            slope = down - up
            u12 = (next_col(slope) - last_col(slope)) * (0.25 * bending)
            old = [out[e, (p - 2) % planes] for e in range(4)]
            new = [out[e, (p - 1) % planes] for e in range(4)]
            bent = [
                u11 * new[0] + u12 * new[2],
                u11 * new[1] + u12 * new[3],
                u12 * new[0] + u22 * new[2],
                u12 * new[1] + u22 * new[3],
            ]
            for e in range(4):
                out[e, p] = (1.0 - mixing) * old[e] + mixing * new[e] - bent[e]
        return carry

    lax.fori_loop(0, g + 1, lens, 0)

    @pl.when(has_high)
    def _():
        halo_copy(0).wait_send()

    @pl.when(has_low)
    def _():
        halo_copy(1).wait_send()

    def coarse_sent(j, carry):
        coarse_copy(j).wait_send()
        return carry

    lax.fori_loop(1, tiles, coarse_sent, 0)

    def later_sent(to, carry):
        later_copy(shorts, short_send, short_recv, to).wait_send()
        later_copy(longs, long_send, long_recv, to).wait_send()
        return carry

    lax.fori_loop(g + 1, groups, later_sent, 0)


def solution(mesh):
    tiles, groups = mesh.shape["tile"], mesh.shape["plane"]

    def body(density, plane_slot, paint_weight, paint_bias, mix_weight, short_kernel):
        planes, rows, cols = density.shape
        channels = paint_weight.shape[0]
        coarse_cols = cols // 4
        vmem = pl.BlockSpec(memory_space=pltpu.VMEM)
        smem = pl.BlockSpec(memory_space=pltpu.SMEM)
        wide = cols + 2 * pad
        dma = pltpu.SemaphoreType.DMA
        return pl.pallas_call(
            functools.partial(kernel, tiles, groups),
            out_shape=jax.ShapeDtypeStruct((4, planes, rows, cols), f32),
            in_specs=[vmem] + [smem] * 5,
            out_specs=vmem,
            scratch_shapes=[
                pltpu.VMEM((3, planes, rows, wide), f32),
                pltpu.VMEM((planes, 16, wide), f32),
                pltpu.VMEM((16 * channels, 240), bf16),
                pltpu.VMEM((16, 240), bf16),
                pltpu.VMEM((coarse_cols, coarse_cols), bf16),
                pltpu.VMEM((coarse_cols, coarse_cols), bf16),
                pltpu.VMEM((128, block), bf16),
                pltpu.VMEM((tiles, 8, coarse_cols), f32),
                pltpu.VMEM((groups, planes + 1, rows, cols), f32),
                pltpu.VMEM((groups, 16, coarse_cols), f32),
                dma((2,)),
                dma((2,)),
                dma((tiles,)),
                dma((tiles,)),
                dma((groups,)),
                dma((groups,)),
                dma((groups,)),
                dma((groups,)),
            ],
            compiler_params=pltpu.CompilerParams(
                collective_id=0, has_side_effects=True, vmem_limit_bytes=48 * 1024 * 1024
            ),
        )(density, plane_slot, paint_weight, paint_bias, mix_weight, short_kernel)

    placed = (P("plane", "tile", None), P(), P(), P(), P(), P())
    return jax.shard_map(
        body, mesh=mesh, in_specs=placed, out_specs=P(None, "plane", "tile", None), check_vma=False
    )
```

```python
import functools
import math

import jax
import jax.numpy as jnp
from jax import lax
from jax.experimental import pallas as pl
from jax.experimental.pallas import tpu as pltpu
from jax.sharding import PartitionSpec as P

lens_gain = 0.25
pad = 128
block = 512
f32 = jnp.float32
bf16 = jnp.bfloat16


def split(x):
    hi = x.astype(bf16)
    return hi, (x - hi.astype(f32)).astype(bf16)


def iota(shape, axis):
    return lax.broadcasted_iota(jnp.int32, shape, axis)


def dot(a, b):
    return jnp.dot(a, b, preferred_element_type=f32)


def kernel(
    tiles, groups, density, slot, weight, bias, mix, short, out,
    ext, conv, paint_lhs, short_lhs, col_hi, col_lo, spread, gathered, shorts, longs,
    own_sem, halo_send, halo_recv, coarse_send, coarse_recv, short_send, short_recv, long_send, long_recv,
):
    planes, rows, cols = density.shape
    channels = weight.shape[1]
    blocks = cols // block
    slots = slot.shape[0]
    coarse_cols = cols // 4
    t = lax.axis_index("tile")
    g = lax.axis_index("plane")

    own_copy = pltpu.make_async_copy(density, ext.at[1, :, :, pl.ds(pad, cols)], own_sem)
    own_copy.start()

    barrier = pltpu.get_barrier_semaphore()

    def greet_tile(j, carry):
        pl.semaphore_signal(barrier, inc=1, device_id={"tile": lax.rem(t + j, tiles)})
        return carry

    def greet_plane(j, carry):
        pl.semaphore_signal(barrier, inc=1, device_id={"plane": lax.rem(g + j, groups)})
        return carry

    lax.fori_loop(1, tiles, greet_tile, 0)
    lax.fori_loop(1, groups, greet_plane, 0)
    pl.semaphore_wait(barrier, tiles + groups - 2)

    def halo_copy(side, cb):
        start = pl.multiple_of(cb * block, block)
        return pltpu.make_async_remote_copy(
            src_ref=density.at[:, :, pl.ds(start, block)],
            dst_ref=ext.at[2 * side, :, :, pl.ds(pl.multiple_of(start + pad, pad), block)],
            send_sem=halo_send.at[side, cb],
            recv_sem=halo_recv.at[side, cb],
            device_id={"tile": lax.rem(t + (1 if side == 0 else tiles - 1), tiles)},
        )

    has_low = t > 0
    has_high = t < tiles - 1

    def halo_start(cb, carry):
        @pl.when(has_high)
        def _():
            halo_copy(0, cb).start()

        @pl.when(has_low)
        def _():
            halo_copy(1, cb).start()

        return carry

    lax.fori_loop(0, blocks, halo_start, 0)

    ext[:, :, :, 0:pad] = jnp.zeros((3, planes, rows, pad), f32)
    ext[:, :, :, pad + cols :] = jnp.zeros((3, planes, rows, pad), f32)
    conv[:, :, 0:pad] = jnp.zeros((planes, 16, pad), f32)
    conv[:, :, pad + cols :] = jnp.zeros((planes, 16, pad), f32)

    @pl.when(jnp.logical_not(has_low))
    def _():
        ext[0, :, :, pad : pad + cols] = jnp.zeros((planes, rows, cols), f32)

    @pl.when(jnp.logical_not(has_high))
    def _():
        ext[2, :, :, pad : pad + cols] = jnp.zeros((planes, rows, cols), f32)

    lane = iota((16, 240), 1)
    sub = iota((16, 240), 0)
    seg = jnp.where(lane >= 160, lane - 160, jnp.where(lane >= 80, lane - 80, lane))
    tap_masks = []
    for i in range(3):
        for j in range(3):
            tap_masks.append(seg == j * 24 + sub + 4 + 2 * (i - 1))

    def pack(value):
        hi = value.astype(bf16).astype(f32)
        return jnp.where(lane < 160, hi, value - hi).astype(bf16)

    def paint_channel(c, carry):
        value = jnp.zeros((16, 240), f32)
        for tap in range(9):
            value = jnp.where(tap_masks[tap], weight[tap, c], value)
        paint_lhs[pl.ds(pl.multiple_of(c * 16, 16), 16), :] = pack(value)
        return carry

    lax.fori_loop(0, channels, paint_channel, 0)

    row_of = jnp.where(sub < 8, sub, jnp.where(sub == 8, -1, 8))
    value = jnp.zeros((16, 240), f32)
    for a in range(5):
        for b in range(5):
            value = jnp.where(
                (seg == b * 16 + row_of + 2 + a) & (sub < 10), short[a, b], value
            )
    short_lhs[...] = pack(value)

    spread[...] = ((iota((128, block), 1) >> 2) == iota((128, block), 0)).astype(f32).astype(bf16)
    pool = ((iota((block, 128), 0) >> 2) == iota((block, 128), 1)).astype(f32).astype(bf16)
    col_scale = cols / 16.0

    def col_rows(i, carry):
        gap = iota((64, coarse_cols), 0) + i * 64 - iota((64, coarse_cols), 1)
        hi, lo = split(jnp.exp(-jnp.abs(gap.astype(f32)) / col_scale))
        at = pl.ds(pl.multiple_of(i * 64, 64), 64)
        col_hi[at, :] = hi
        col_lo[at, :] = lo
        return carry

    lax.fori_loop(0, coarse_cols // 64, col_rows, 0)

    def halo_wait(cb):
        @pl.when(has_low)
        def _():
            halo_copy(0, cb).wait_recv()

        @pl.when(has_high)
        def _():
            halo_copy(1, cb).wait_recv()

    own_copy.wait()
    halo_wait(0)

    row_global = iota((16, block), 0) + (t * rows - 4)
    row_real = (row_global >= 0) & (row_global < tiles * rows)

    def paint(cb):
        window = pl.ds(pl.multiple_of(cb * block, block), block + 2 * pad)
        sums = []
        for p in range(planes):
            parts = [ext[s, p, :, window] for s in range(3)]
            stacked = []
            for j in range(3):
                start = pad + 2 * (j - 1)
                stacked += [part[:, start : start + block] for part in parts]
            stacked.append(jnp.zeros((8, block), f32))
            hi, lo = split(jnp.concatenate(stacked, axis=0))
            pre = dot(paint_lhs[...], jnp.concatenate([hi, lo, hi], axis=0))
            total = jnp.zeros((16, block), f32)
            for c in range(channels):
                total += mix[c] * jnp.tanh(pre[16 * c : 16 * c + 16] + bias[c])
            total = jnp.where(row_real, total, 0.0)
            conv[p, :, pl.ds(pl.multiple_of(cb * block + pad, pad), block)] = total
            sums.append(jnp.sum(total[4:8], axis=0, keepdims=True))
            sums.append(jnp.sum(total[8:12], axis=0, keepdims=True))
        sums += [jnp.zeros((1, block), f32)] * (8 - 2 * planes)
        hi, lo = split(jnp.concatenate(sums, axis=0) * (1.0 / 16.0))
        coarse = dot(hi, pool) + dot(lo, pool)
        gathered[t, :, pl.ds(pl.multiple_of(cb * 128, 128), 128)] = coarse

    def short_copy(cb, to):
        at = pl.ds(pl.multiple_of(cb * block, block), block)
        return pltpu.make_async_remote_copy(
            src_ref=shorts.at[g, :, :, at],
            dst_ref=shorts.at[g, :, :, at],
            send_sem=short_send.at[to, cb],
            recv_sem=short_recv.at[g, cb],
            device_id={"plane": to},
        )

    def long_copy(to):
        return pltpu.make_async_remote_copy(
            src_ref=longs.at[g],
            dst_ref=longs.at[g],
            send_sem=long_send.at[to],
            recv_sem=long_recv.at[g],
            device_id={"plane": to},
        )

    def short_block(cb):
        window = pl.ds(pl.multiple_of(cb * block, block), block + 2 * pad)
        at = pl.ds(pl.multiple_of(cb * block, block), block)
        edges = []
        for p in range(planes):
            part = conv[p, :, window]
            stacked = [part[:, pad + b - 2 : pad + b - 2 + block] for b in range(5)]
            hi, lo = split(jnp.concatenate(stacked, axis=0))
            value = dot(short_lhs[...], jnp.concatenate([hi, lo, hi], axis=0))
            shorts[g, p, :, at] = value[0:8]
            edges.append(value[8:10])
        edges += [jnp.zeros((8 - 2 * planes, block), f32)]
        shorts[g, planes, :, at] = jnp.concatenate(edges, axis=0)

        def short_start(to, carry):
            short_copy(cb, to).start()
            return carry

        lax.fori_loop(g + 1, groups, short_start, 0)

    def coarse_copy(j):
        return pltpu.make_async_remote_copy(
            src_ref=gathered.at[t],
            dst_ref=gathered.at[t],
            send_sem=coarse_send.at[j],
            recv_sem=coarse_recv.at[t],
            device_id={"tile": lax.rem(t + j, tiles)},
        )

    def coarse_start(j, carry):
        coarse_copy(j).start()
        return carry

    def paint_step(cb, carry):
        @pl.when(cb + 1 < blocks)
        def _():
            halo_wait(cb + 1)

        paint(cb)

        @pl.when(cb > 0)
        def _():
            short_block(cb - 1)

        return carry

    lax.fori_loop(0, blocks, paint_step, 0)
    lax.fori_loop(1, tiles, coarse_start, 0)
    short_block(blocks - 1)

    def coarse_wait(j, carry):
        source = lax.rem(t + j, tiles)
        pltpu.make_async_remote_copy(
            src_ref=gathered.at[source],
            dst_ref=gathered.at[source],
            send_sem=coarse_send.at[j],
            recv_sem=coarse_recv.at[source],
            device_id={"tile": source},
        ).wait_recv()
        return carry

    lax.fori_loop(1, tiles, coarse_wait, 0)
    row_scale = tiles * rows / 16.0
    long_gain = 1.0 / math.sqrt(row_scale * col_scale)
    m = iota((16, tiles * 8), 0)
    n = iota((16, tiles * 8), 1)
    gap = (2 * t - 1 + (m & 3)) - (2 * (n >> 3) + (n & 1))
    near = jnp.exp(-jnp.abs(gap.astype(f32)) / row_scale) * long_gain
    row_kernel = jnp.where((m >> 2) == ((n & 7) >> 1), near, 0.0)
    everything = gathered[...].reshape(tiles * 8, coarse_cols)
    row_hi, row_lo = split(row_kernel)
    hi, lo = split(everything)
    summed = dot(
        jnp.concatenate([row_hi, row_hi, row_lo], axis=1), jnp.concatenate([hi, lo, hi], axis=0)
    )
    hi, lo = split(summed)
    both = dot(jnp.concatenate([hi, lo], axis=0), col_hi[...])
    longs[g] = both[0:16] + both[16:32] + dot(hi, col_lo[...])

    def long_start(to, carry):
        long_copy(to).start()
        return carry

    lax.fori_loop(g + 1, groups, long_start, 0)

    for entry in range(4):
        for p in (planes - 2, planes - 1):
            out[entry, p] = jnp.full((rows, cols), 1.0 if entry in (0, 3) else 0.0, f32)
    row_at = iota((rows, cols), 0)
    col_at = iota((rows, cols), 1)
    low_gain = jnp.where(t > 0, 1.0, 0.0)
    high_gain = jnp.where(t < tiles - 1, 1.0, 0.0)
    slot_total = 2.0 * slots
    wide = cols // 128

    def next_col(x):
        return jnp.where(col_at == cols - 1, 0.0, pltpu.roll(x, cols - 1, 1))

    def last_col(x):
        return jnp.where(col_at == 0, 0.0, pltpu.roll(x, 1, 1))

    def lens(gi, carry):
        @pl.when(gi < g)
        def _():
            def short_wait(cb, carry):
                at = pl.ds(pl.multiple_of(cb * block, block), block)
                pltpu.make_async_remote_copy(
                    src_ref=shorts.at[gi, :, :, at],
                    dst_ref=shorts.at[gi, :, :, at],
                    send_sem=short_send.at[gi, cb],
                    recv_sem=short_recv.at[gi, cb],
                    device_id={"plane": gi},
                ).wait_recv()
                return carry

            lax.fori_loop(0, blocks, short_wait, 0)
            pltpu.make_async_remote_copy(
                src_ref=longs.at[gi],
                dst_ref=longs.at[gi],
                send_sem=long_send.at[gi],
                recv_sem=long_recv.at[gi],
                device_id={"plane": gi},
            ).wait_recv()

        hi, lo = split(longs[gi])
        pieces = coarse_cols // 128
        stacked = [x[:, 128 * b : 128 * b + 128] for x in (hi, lo) for b in range(pieces)]
        spread_out = dot(jnp.concatenate(stacked, axis=0), spread[...])
        upper = [
            spread_out[16 * b : 16 * b + 16]
            + spread_out[16 * (pieces + b) : 16 * (pieces + b) + 16]
            for b in range(pieces)
        ]
        long_wide = jnp.concatenate(upper, axis=1)
        edges = shorts[gi, planes]
        for p in range(planes):
            k = gi * planes + p

            def distance(index):
                value = jnp.full((8, 128), slot[index], jnp.int32)
                return (value.astype(f32) + 1.0) / slot_total

            here = distance(k)
            before = jnp.where(k > 0, distance(jnp.maximum(k - 1, 0)), 0.0)
            after = jnp.where(
                k < slots - 1,
                distance(jnp.minimum(k + 1, slots - 1)),
                (slot_total + 1.0) / slot_total,
            )
            mixing = before * (after - here) / (here * (after - before))
            bending = lens_gain * (after - here) / after
            mixing = jnp.concatenate([mixing] * wide, axis=1)
            bending = jnp.concatenate([bending] * wide, axis=1)
            center = shorts[gi, p] + jnp.where(
                row_at < 4, long_wide[4 * p + 1 : 4 * p + 2], long_wide[4 * p + 2 : 4 * p + 3]
            )
            top = (edges[2 * p : 2 * p + 1] + long_wide[4 * p : 4 * p + 1]) * low_gain
            bottom = (
                edges[2 * p + 1 : 2 * p + 2] + long_wide[4 * p + 3 : 4 * p + 4]
            ) * high_gain
            up = jnp.where(row_at == 0, top, pltpu.roll(center, 1, 0))
            down = jnp.where(row_at == rows - 1, bottom, pltpu.roll(center, rows - 1, 0))
            u11 = (down - 2.0 * center + up) * bending
            u22 = (next_col(center) - 2.0 * center + last_col(center)) * bending
            slope = down - up
            u12 = (next_col(slope) - last_col(slope)) * (0.25 * bending)
            old = [out[e, (p - 2) % planes] for e in range(4)]
            new = [out[e, (p - 1) % planes] for e in range(4)]
            bent = [
                u11 * new[0] + u12 * new[2],
                u11 * new[1] + u12 * new[3],
                u12 * new[0] + u22 * new[2],
                u12 * new[1] + u22 * new[3],
            ]
            for e in range(4):
                out[e, p] = (1.0 - mixing) * old[e] + mixing * new[e] - bent[e]
        return carry

    lax.fori_loop(0, g + 1, lens, 0)

    def halo_sent(cb, carry):
        @pl.when(has_high)
        def _():
            halo_copy(0, cb).wait_send()

        @pl.when(has_low)
        def _():
            halo_copy(1, cb).wait_send()

        return carry

    lax.fori_loop(0, blocks, halo_sent, 0)

    def coarse_sent(j, carry):
        coarse_copy(j).wait_send()
        return carry

    lax.fori_loop(1, tiles, coarse_sent, 0)

    def later_sent(to, carry):
        def block_sent(cb, inner):
            short_copy(cb, to).wait_send()
            return inner

        lax.fori_loop(0, blocks, block_sent, 0)
        long_copy(to).wait_send()
        return carry

    lax.fori_loop(g + 1, groups, later_sent, 0)


def solution(mesh):
    tiles, groups = mesh.shape["tile"], mesh.shape["plane"]

    def body(density, plane_slot, paint_weight, paint_bias, mix_weight, short_kernel):
        planes, rows, cols = density.shape
        channels = paint_weight.shape[0]
        coarse_cols = cols // 4
        blocks = cols // block
        vmem = pl.BlockSpec(memory_space=pltpu.VMEM)
        smem = pl.BlockSpec(memory_space=pltpu.SMEM)
        wide = cols + 2 * pad
        dma = pltpu.SemaphoreType.DMA
        return pl.pallas_call(
            functools.partial(kernel, tiles, groups),
            out_shape=jax.ShapeDtypeStruct((4, planes, rows, cols), f32),
            in_specs=[pl.BlockSpec(memory_space=pltpu.HBM)] + [smem] * 5,
            out_specs=vmem,
            scratch_shapes=[
                pltpu.VMEM((3, planes, rows, wide), f32),
                pltpu.VMEM((planes, 16, wide), f32),
                pltpu.VMEM((16 * channels, 240), bf16),
                pltpu.VMEM((16, 240), bf16),
                pltpu.VMEM((coarse_cols, coarse_cols), bf16),
                pltpu.VMEM((coarse_cols, coarse_cols), bf16),
                pltpu.VMEM((128, block), bf16),
                pltpu.VMEM((tiles, 8, coarse_cols), f32),
                pltpu.VMEM((groups, planes + 1, rows, cols), f32),
                pltpu.VMEM((groups, 16, coarse_cols), f32),
                dma(()),
                dma((2, blocks)),
                dma((2, blocks)),
                dma((tiles,)),
                dma((tiles,)),
                dma((groups, blocks)),
                dma((groups, blocks)),
                dma((groups,)),
                dma((groups,)),
            ],
            compiler_params=pltpu.CompilerParams(
                collective_id=0, has_side_effects=True, vmem_limit_bytes=48 * 1024 * 1024
            ),
        )(density, plane_slot, paint_weight.T, paint_bias, mix_weight, short_kernel)

    placed = (P("plane", "tile", None), P(), P(), P(), P(), P())
    return jax.shard_map(
        body, mesh=mesh, in_specs=placed, out_specs=P(None, "plane", "tile", None), check_vma=False
    )
```

```python
import functools
import math

import jax
import jax.numpy as jnp
from jax import lax
from jax.experimental import pallas as pl
from jax.experimental.pallas import tpu as pltpu
from jax.sharding import PartitionSpec as P

lens_gain = 0.25
pad = 128
block = 512
f32 = jnp.float32
bf16 = jnp.bfloat16


def split(x):
    hi = x.astype(bf16)
    return hi, (x - hi.astype(f32)).astype(bf16)


def iota(shape, axis):
    return lax.broadcasted_iota(jnp.int32, shape, axis)


def dot(a, b):
    return jnp.dot(a, b, preferred_element_type=f32)


def kernel(
    tiles, groups, density, slot, weight, bias, mix, short, out,
    mass_own, mass_edge, conv_own, conv_edge, paint_lhs, short_lhs, col_hi, col_lo, spread,
    gathered, shorts, longs, long_wide, state,
    own_sem, out_sem, mass_send, mass_recv, conv_send, conv_recv, coarse_send, coarse_recv,
    short_send, short_recv, long_send, long_recv,
):
    planes, rows, cols = density.shape
    channels = weight.shape[1]
    blocks = cols // block
    slots = slot.shape[0]
    coarse_cols = cols // 4
    half = rows // 2
    t = lax.axis_index("tile")
    g = lax.axis_index("plane")
    has_low = t > 0
    has_high = t < tiles - 1

    def at_block(cb):
        return pl.ds(pl.multiple_of(cb * block, block), block)

    def at_padded(cb):
        return pl.ds(pl.multiple_of(cb * block + pad, pad), block)

    def at_window(cb):
        return pl.ds(pl.multiple_of(cb * block, block), block + 2 * pad)

    own_copy = pltpu.make_async_copy(density, mass_own.at[:, :, pl.ds(pad, cols)], own_sem)
    own_copy.start()

    barrier = pltpu.get_barrier_semaphore()

    def greet_tile(j, carry):
        pl.semaphore_signal(barrier, inc=1, device_id={"tile": lax.rem(t + j, tiles)})
        return carry

    def greet_plane(j, carry):
        pl.semaphore_signal(barrier, inc=1, device_id={"plane": lax.rem(g + j, groups)})
        return carry

    lax.fori_loop(1, tiles, greet_tile, 0)
    lax.fori_loop(1, groups, greet_plane, 0)
    pl.semaphore_wait(barrier, tiles + groups - 2)

    def edge_copy(source, source_at, target, send, recv, side, cb):
        take = pl.ds(half, half) if side == 0 else pl.ds(0, half)
        give = pl.ds(0, half) if side == 0 else pl.ds(half, half)
        return pltpu.make_async_remote_copy(
            src_ref=source.at[:, take, source_at(cb)],
            dst_ref=target.at[:, give, at_padded(cb)],
            send_sem=send.at[side, cb],
            recv_sem=recv.at[side, cb],
            device_id={"tile": lax.rem(t + (1 if side == 0 else tiles - 1), tiles)},
        )

    def mass_copy(side, cb):
        return edge_copy(density, at_block, mass_edge, mass_send, mass_recv, side, cb)

    def conv_copy(side, cb):
        return edge_copy(conv_own, at_padded, conv_edge, conv_send, conv_recv, side, cb)

    def edge_start(copy, cb):
        @pl.when(has_high)
        def _():
            copy(0, cb).start()

        @pl.when(has_low)
        def _():
            copy(1, cb).start()

    def edge_wait(copy, cb):
        @pl.when(has_low)
        def _():
            copy(0, cb).wait_recv()

        @pl.when(has_high)
        def _():
            copy(1, cb).wait_recv()

    def edge_sent(copy, cb):
        @pl.when(has_high)
        def _():
            copy(0, cb).wait_send()

        @pl.when(has_low)
        def _():
            copy(1, cb).wait_send()

    def mass_start(cb, carry):
        edge_start(mass_copy, cb)
        return carry

    lax.fori_loop(0, blocks, mass_start, 0)

    for buffer in (mass_own, mass_edge, conv_own, conv_edge):
        buffer[:, :, 0:pad] = jnp.zeros((planes, rows, pad), f32)
        buffer[:, :, pad + cols :] = jnp.zeros((planes, rows, pad), f32)
    for buffer in (mass_edge, conv_edge):

        @pl.when(jnp.logical_not(has_low))
        def _():
            buffer[:, 0:half, pad : pad + cols] = jnp.zeros((planes, half, cols), f32)

        @pl.when(jnp.logical_not(has_high))
        def _():
            buffer[:, half:rows, pad : pad + cols] = jnp.zeros((planes, half, cols), f32)

    shorts[:, :, :, 0:pad] = jnp.zeros((groups, planes + 1, rows, pad), f32)
    shorts[:, :, :, pad + cols :] = jnp.zeros((groups, planes + 1, rows, pad), f32)
    long_wide[:, 0:pad] = jnp.zeros((16, pad), f32)
    long_wide[:, pad + cols :] = jnp.zeros((16, pad), f32)

    def row_of_place(place):
        return jnp.where(place < half, place - half, jnp.where(place < rows, place + half, place - rows))

    def pack(value, lane, size):
        hi = value.astype(bf16).astype(f32)
        return jnp.where(lane < 2 * size, hi, value - hi).astype(bf16)

    lane = iota((16, 192), 1)
    sub = iota((16, 192), 0)
    seg = lane & 63
    part = seg >> 4
    step = row_of_place(seg & 15) - (sub & 7)
    tap_masks = []
    for i in range(3):
        for j in range(3):
            tap_masks.append((part == j) & (step == 2 * (i - 1)))
    bias_mask = seg == 48
    first = sub < 8

    def paint_pair(c, carry):
        value = jnp.where(bias_mask, jnp.where(first, bias[2 * c], bias[2 * c + 1]), 0.0)
        for tap in range(9):
            pair = jnp.where(first, weight[tap, 2 * c], weight[tap, 2 * c + 1])
            value = jnp.where(tap_masks[tap], pair, value)
        paint_lhs[pl.ds(pl.multiple_of(c * 16, 16), 16), :] = pack(value, lane, 64)
        return carry

    lax.fori_loop(0, channels // 2, paint_pair, 0)
    one_row = jnp.where(iota((16, block), 0) == 0, 1.0, 0.0).astype(f32)

    lane = iota((16, 240), 1)
    sub = iota((16, 240), 0)
    seg = jnp.where(lane >= 160, lane - 160, jnp.where(lane >= 80, lane - 80, lane))
    part = seg >> 4
    step = row_of_place(seg & 15) - jnp.where(sub < 8, sub, jnp.where(sub == 8, -1, 8))
    value = jnp.zeros((16, 240), f32)
    for a in range(5):
        for b in range(5):
            value = jnp.where((part == b) & (step == a - 2) & (sub < 10), short[a, b], value)
    short_lhs[...] = pack(value, lane, 80)

    spread[...] = ((iota((128, block), 1) >> 2) == iota((128, block), 0)).astype(f32).astype(bf16)
    pool = ((iota((block, 128), 0) >> 2) == iota((block, 128), 1)).astype(f32).astype(bf16)
    col_scale = cols / 16.0

    def col_rows(i, carry):
        gap = iota((64, coarse_cols), 0) + i * 64 - iota((64, coarse_cols), 1)
        hi, lo = split(jnp.exp(-jnp.abs(gap.astype(f32)) / col_scale))
        at = pl.ds(pl.multiple_of(i * 64, 64), 64)
        col_hi[at, :] = hi
        col_lo[at, :] = lo
        return carry

    lax.fori_loop(0, coarse_cols // 64, col_rows, 0)
    own_copy.wait()
    edge_wait(mass_copy, 0)

    def paint(cb):
        sums = []
        for p in range(planes):
            parts = [mass_edge[p, :, at_window(cb)], mass_own[p, :, at_window(cb)]]
            stacked = []
            for j in range(3):
                start = pad + 2 * (j - 1)
                stacked += [x[:, start : start + block] for x in parts]
            stacked.append(one_row)
            hi, lo = split(jnp.concatenate(stacked, axis=0))
            pre = dot(paint_lhs[...], jnp.concatenate([hi, lo, hi], axis=0))
            total = jnp.zeros((rows, block), f32)
            for c in range(channels):
                total += mix[c] * jnp.tanh(pre[rows * c : rows * c + rows])
            conv_own[p, :, at_padded(cb)] = total
            sums.append(jnp.sum(total[0:4], axis=0, keepdims=True))
            sums.append(jnp.sum(total[4:8], axis=0, keepdims=True))
        sums += [jnp.zeros((1, block), f32)] * (8 - 2 * planes)
        hi, lo = split(jnp.concatenate(sums, axis=0) * (1.0 / 16.0))
        coarse = dot(hi, pool) + dot(lo, pool)
        gathered[t, :, pl.ds(pl.multiple_of(cb * 128, 128), 128)] = coarse

    def short_copy(cb, to):
        return pltpu.make_async_remote_copy(
            src_ref=shorts.at[g, :, :, at_padded(cb)],
            dst_ref=shorts.at[g, :, :, at_padded(cb)],
            send_sem=short_send.at[to, cb],
            recv_sem=short_recv.at[g, cb],
            device_id={"plane": to},
        )

    def long_copy(to):
        return pltpu.make_async_remote_copy(
            src_ref=longs.at[g],
            dst_ref=longs.at[g],
            send_sem=long_send.at[to],
            recv_sem=long_recv.at[g],
            device_id={"plane": to},
        )

    def short_block(cb):
        edges = []
        for p in range(planes):
            parts = [conv_edge[p, :, at_window(cb)], conv_own[p, :, at_window(cb)]]
            stacked = [
                x[:, pad + b - 2 : pad + b - 2 + block] for b in range(5) for x in parts
            ]
            hi, lo = split(jnp.concatenate(stacked, axis=0))
            value = dot(short_lhs[...], jnp.concatenate([hi, lo, hi], axis=0))
            shorts[g, p, :, at_padded(cb)] = value[0:8]
            edges.append(value[8:10])
        edges += [jnp.zeros((8 - 2 * planes, block), f32)]
        shorts[g, planes, :, at_padded(cb)] = jnp.concatenate(edges, axis=0)

        def short_start(to, carry):
            short_copy(cb, to).start()
            return carry

        lax.fori_loop(g + 1, groups, short_start, 0)

    def coarse_copy(j):
        return pltpu.make_async_remote_copy(
            src_ref=gathered.at[t],
            dst_ref=gathered.at[t],
            send_sem=coarse_send.at[j],
            recv_sem=coarse_recv.at[t],
            device_id={"tile": lax.rem(t + j, tiles)},
        )

    def coarse_start(j, carry):
        coarse_copy(j).start()
        return carry

    def paint_step(cb, carry):
        @pl.when(cb + 1 < blocks)
        def _():
            edge_wait(mass_copy, cb + 1)

        paint(cb)

        @pl.when(cb + 1 < blocks)
        def _():
            edge_start(conv_copy, cb)

        @pl.when(cb == 2)
        def _():
            edge_wait(conv_copy, 0)

        @pl.when(cb > 1)
        def _():
            edge_wait(conv_copy, cb - 1)
            short_block(cb - 2)

        return carry

    lax.fori_loop(0, blocks, paint_step, 0)
    lax.fori_loop(1, tiles, coarse_start, 0)
    edge_start(conv_copy, blocks - 1)
    short_rest = max(blocks - 2, 0)

    def short_step(cb, carry):
        @pl.when(cb + 1 < blocks)
        def _():
            edge_wait(conv_copy, cb + 1)

        short_block(cb)
        return carry

    lax.fori_loop(short_rest, blocks, short_step, 0)

    def coarse_wait(j, carry):
        source = lax.rem(t + j, tiles)
        pltpu.make_async_remote_copy(
            src_ref=gathered.at[source],
            dst_ref=gathered.at[source],
            send_sem=coarse_send.at[j],
            recv_sem=coarse_recv.at[source],
            device_id={"tile": source},
        ).wait_recv()
        return carry

    row_scale = tiles * rows / 16.0
    long_gain = 1.0 / math.sqrt(row_scale * col_scale)
    m = iota((16, tiles * 8), 0)
    n = iota((16, tiles * 8), 1)
    gap = (2 * t - 1 + (m & 3)) - (2 * (n >> 3) + (n & 1))
    near = jnp.exp(-jnp.abs(gap.astype(f32)) / row_scale) * long_gain
    row_kernel = jnp.where((m >> 2) == ((n & 7) >> 1), near, 0.0)
    row_hi, row_lo = split(row_kernel)
    row_lhs = jnp.concatenate([row_hi, row_hi, row_lo], axis=1)
    lax.fori_loop(1, tiles, coarse_wait, 0)
    hi, lo = split(gathered[...].reshape(tiles * 8, coarse_cols))
    hi, lo = split(dot(row_lhs, jnp.concatenate([hi, lo, hi], axis=0)))
    both = dot(jnp.concatenate([hi, lo], axis=0), col_hi[...])
    longs[g] = both[0:16] + both[16:32] + dot(hi, col_lo[...])

    def long_start(to, carry):
        long_copy(to).start()
        return carry

    lax.fori_loop(g + 1, groups, long_start, 0)

    for entry in range(4):
        for p in (planes - 2, planes - 1):
            state[entry, p] = jnp.full((rows, cols), 1.0 if entry in (0, 3) else 0.0, f32)
    row_at = iota((rows, block + 2 * pad), 0)
    low_gain = jnp.where(t > 0, 1.0, 0.0)
    high_gain = jnp.where(t < tiles - 1, 1.0, 0.0)
    slot_total = 2.0 * slots
    pieces = coarse_cols // 128

    def out_copy(cb):
        return pltpu.make_async_copy(
            state.at[:, :, :, at_block(cb)], out.at[:, :, :, at_block(cb)], out_sem.at[cb]
        )

    def lens(gi, carry):
        @pl.when(gi < g)
        def _():
            def short_wait(cb, inner):
                pltpu.make_async_remote_copy(
                    src_ref=shorts.at[gi, :, :, at_padded(cb)],
                    dst_ref=shorts.at[gi, :, :, at_padded(cb)],
                    send_sem=short_send.at[gi, cb],
                    recv_sem=short_recv.at[gi, cb],
                    device_id={"plane": gi},
                ).wait_recv()
                return inner

            lax.fori_loop(0, blocks, short_wait, 0)
            pltpu.make_async_remote_copy(
                src_ref=longs.at[gi],
                dst_ref=longs.at[gi],
                send_sem=long_send.at[gi],
                recv_sem=long_recv.at[gi],
                device_id={"plane": gi},
            ).wait_recv()

        hi, lo = split(longs[gi])
        stacked = [x[:, 128 * b : 128 * b + 128] for x in (hi, lo) for b in range(pieces)]
        spread_out = dot(jnp.concatenate(stacked, axis=0), spread[...])
        for b in range(pieces):
            long_wide[:, pad + b * block : pad + b * block + block] = (
                spread_out[16 * b : 16 * b + 16]
                + spread_out[16 * (pieces + b) : 16 * (pieces + b) + 16]
            )

        factors = []
        for p in range(planes):
            k = gi * planes + p

            def distance(index):
                value = jnp.full((8, 128), slot[index], jnp.int32)
                return (value.astype(f32) + 1.0) / slot_total

            here = distance(k)
            before = jnp.where(k > 0, distance(jnp.maximum(k - 1, 0)), 0.0)
            after = jnp.where(
                k < slots - 1,
                distance(jnp.minimum(k + 1, slots - 1)),
                (slot_total + 1.0) / slot_total,
            )
            mixing = before * (after - here) / (here * (after - before))
            bending = lens_gain * (after - here) / after
            factors.append((mixing, bending))

        def lens_block(cb, inner):
            at = at_block(cb)
            edges = shorts[gi, planes, :, at_window(cb)]
            longer = long_wide[:, at_window(cb)]
            old = [state[e, planes - 2, :, at] for e in range(4)]
            new = [state[e, planes - 1, :, at] for e in range(4)]
            for p in range(planes):
                mixing, bending = [
                    jnp.concatenate([x] * (block // 128), axis=1) for x in factors[p]
                ]
                center = shorts[gi, p, :, at_window(cb)] + jnp.where(
                    row_at < 4, longer[4 * p + 1 : 4 * p + 2], longer[4 * p + 2 : 4 * p + 3]
                )
                top = (edges[2 * p : 2 * p + 1] + longer[4 * p : 4 * p + 1]) * low_gain
                bottom = (
                    edges[2 * p + 1 : 2 * p + 2] + longer[4 * p + 3 : 4 * p + 4]
                ) * high_gain
                up = jnp.where(row_at == 0, top, pltpu.roll(center, 1, 0))
                down = jnp.where(row_at == rows - 1, bottom, pltpu.roll(center, rows - 1, 0))

                def moved(x, by):
                    return x[:, pad + by : pad + by + block]

                here = moved(center, 0) * 2.0
                slope = down - up
                u11 = (moved(down, 0) + moved(up, 0) - here) * bending
                u22 = (moved(center, 1) + moved(center, -1) - here) * bending
                u12 = (moved(slope, 1) - moved(slope, -1)) * (0.25 * bending)
                bent = [
                    u11 * new[0] + u12 * new[2],
                    u11 * new[1] + u12 * new[3],
                    u12 * new[0] + u22 * new[2],
                    u12 * new[1] + u22 * new[3],
                ]
                keep = 1.0 - mixing
                advanced = [keep * old[e] + mixing * new[e] - bent[e] for e in range(4)]
                for e in range(4):
                    state[e, p, :, at] = advanced[e]
                old, new = new, advanced

            @pl.when(gi == g)
            def _():
                out_copy(cb).start()

            return inner

        lax.fori_loop(0, blocks, lens_block, 0)
        return carry

    lax.fori_loop(0, g + 1, lens, 0)

    def block_sent(cb, carry):
        edge_sent(mass_copy, cb)
        edge_sent(conv_copy, cb)
        return carry

    lax.fori_loop(0, blocks, block_sent, 0)

    def coarse_sent(j, carry):
        coarse_copy(j).wait_send()
        return carry

    lax.fori_loop(1, tiles, coarse_sent, 0)

    def later_sent(to, carry):
        def short_sent(cb, inner):
            short_copy(cb, to).wait_send()
            return inner

        lax.fori_loop(0, blocks, short_sent, 0)
        long_copy(to).wait_send()
        return carry

    lax.fori_loop(g + 1, groups, later_sent, 0)

    def out_done(cb, carry):
        out_copy(cb).wait()
        return carry

    lax.fori_loop(0, blocks, out_done, 0)


def solution(mesh):
    tiles, groups = mesh.shape["tile"], mesh.shape["plane"]

    def body(density, plane_slot, paint_weight, paint_bias, mix_weight, short_kernel):
        planes, rows, cols = density.shape
        channels = paint_weight.shape[0]
        coarse_cols = cols // 4
        blocks = cols // block
        place = pl.BlockSpec(memory_space=pltpu.HBM)
        smem = pl.BlockSpec(memory_space=pltpu.SMEM)
        wide = cols + 2 * pad
        dma = pltpu.SemaphoreType.DMA
        map_shape = pltpu.VMEM((planes, rows, wide), f32)
        return pl.pallas_call(
            functools.partial(kernel, tiles, groups),
            out_shape=jax.ShapeDtypeStruct((4, planes, rows, cols), f32),
            in_specs=[place] + [smem] * 5,
            out_specs=place,
            scratch_shapes=[
                map_shape,
                map_shape,
                map_shape,
                map_shape,
                pltpu.VMEM((8 * channels, 192), bf16),
                pltpu.VMEM((16, 240), bf16),
                pltpu.VMEM((coarse_cols, coarse_cols), bf16),
                pltpu.VMEM((coarse_cols, coarse_cols), bf16),
                pltpu.VMEM((128, block), bf16),
                pltpu.VMEM((tiles, 8, coarse_cols), f32),
                pltpu.VMEM((groups, planes + 1, rows, wide), f32),
                pltpu.VMEM((groups, 16, coarse_cols), f32),
                pltpu.VMEM((16, wide), f32),
                pltpu.VMEM((4, planes, rows, cols), f32),
                dma(()),
                dma((blocks,)),
                dma((2, blocks)),
                dma((2, blocks)),
                dma((2, blocks)),
                dma((2, blocks)),
                dma((tiles,)),
                dma((tiles,)),
                dma((groups, blocks)),
                dma((groups, blocks)),
                dma((groups,)),
                dma((groups,)),
            ],
            compiler_params=pltpu.CompilerParams(
                collective_id=0, has_side_effects=True, vmem_limit_bytes=60 * 1024 * 1024
            ),
        )(density, plane_slot, paint_weight.T, paint_bias, mix_weight, short_kernel)

    placed = (P("plane", "tile", None), P(), P(), P(), P(), P())
    return jax.shard_map(
        body, mesh=mesh, in_specs=placed, out_specs=P(None, "plane", "tile", None), check_vma=False
    )
```

```python
import functools
import math

import jax
import jax.numpy as jnp
from jax import lax
from jax.experimental import pallas as pl
from jax.experimental.pallas import tpu as pltpu
from jax.sharding import PartitionSpec as P

lens_gain = 0.25
pad = 128
block = 512
f32 = jnp.float32
bf16 = jnp.bfloat16


def split(x):
    hi = x.astype(bf16)
    return hi, (x - hi.astype(f32)).astype(bf16)


def iota(shape, axis):
    return lax.broadcasted_iota(jnp.int32, shape, axis)


def dot(a, b):
    return jnp.dot(a, b, preferred_element_type=f32)


def kernel(
    tiles, groups, density, slot, weight, bias, mix, short, out,
    mass_own, mass_edge, conv_own, conv_edge, paint_lhs, short_lhs, col_hi, col_lo, spread,
    gathered, shorts, longs,
    mass_send, mass_recv, conv_send, conv_recv, coarse_send, coarse_recv,
    short_send, short_recv, long_send, long_recv,
):
    planes, rows, cols = density.shape
    channels = weight.shape[0]
    slots = slot.shape[0]
    blocks = cols // block
    coarse_cols = cols // 4
    half = rows // 2
    t = lax.axis_index("tile")
    g = lax.axis_index("plane")
    has_low = t > 0
    has_high = t < tiles - 1

    def at_block(cb):
        return pl.ds(pl.multiple_of(cb * block, block), block)

    def at_padded(cb):
        return pl.ds(pl.multiple_of(cb * block + pad, pad), block)

    def at_window(cb):
        return pl.ds(pl.multiple_of(cb * block, block), block + 2 * pad)

    def shifted(x, by):
        moved = x if by == 0 else pltpu.roll(x, (-by) % (block + 2 * pad), 1)
        return moved[:, pad : pad + block]

    barrier = pltpu.get_barrier_semaphore()

    def greet_tile(j, carry):
        pl.semaphore_signal(barrier, inc=1, device_id={"tile": lax.rem(t + j, tiles)})
        return carry

    def greet_plane(j, carry):
        pl.semaphore_signal(barrier, inc=1, device_id={"plane": lax.rem(g + j, groups)})
        return carry

    lax.fori_loop(1, tiles, greet_tile, 0)
    lax.fori_loop(1, groups, greet_plane, 0)
    pl.semaphore_wait(barrier, tiles + groups - 2)

    def edge_copy(source, source_at, target, send, recv, side, cb):
        take = pl.ds(half, half) if side == 0 else pl.ds(0, half)
        give = pl.ds(0, half) if side == 0 else pl.ds(half, half)
        return pltpu.make_async_remote_copy(
            src_ref=source.at[:, take, source_at(cb)],
            dst_ref=target.at[:, give, at_padded(cb)],
            send_sem=send.at[side, cb],
            recv_sem=recv.at[side, cb],
            device_id={"tile": lax.rem(t + (1 if side == 0 else tiles - 1), tiles)},
        )

    def mass_copy(side, cb):
        return edge_copy(density, at_block, mass_edge, mass_send, mass_recv, side, cb)

    def conv_copy(side, cb):
        return edge_copy(conv_own, at_padded, conv_edge, conv_send, conv_recv, side, cb)

    def edge_start(copy, cb):
        @pl.when(has_high)
        def _():
            copy(0, cb).start()

        @pl.when(has_low)
        def _():
            copy(1, cb).start()

    def edge_wait(copy, cb):
        @pl.when(has_low)
        def _():
            copy(0, cb).wait_recv()

        @pl.when(has_high)
        def _():
            copy(1, cb).wait_recv()

    def edge_sent(copy, cb):
        @pl.when(has_high)
        def _():
            copy(0, cb).wait_send()

        @pl.when(has_low)
        def _():
            copy(1, cb).wait_send()

    def mass_start(cb, carry):
        edge_start(mass_copy, cb)
        return carry

    lax.fori_loop(0, blocks, mass_start, 0)

    for buffer in (mass_own, mass_edge, conv_own, conv_edge):
        buffer[:, :, 0:pad] = jnp.zeros((planes, rows, pad), f32)
        buffer[:, :, pad + cols :] = jnp.zeros((planes, rows, pad), f32)
    for buffer in (mass_edge, conv_edge):

        @pl.when(jnp.logical_not(has_low))
        def _():
            buffer[:, 0:half, pad : pad + cols] = jnp.zeros((planes, half, cols), f32)

        @pl.when(jnp.logical_not(has_high))
        def _():
            buffer[:, half:rows, pad : pad + cols] = jnp.zeros((planes, half, cols), f32)

    def row_of_place(place):
        return jnp.where(place < half, place - half, jnp.where(place < rows, place + half, place - rows))

    def pack(value, lane, size):
        hi = value.astype(bf16).astype(f32)
        return jnp.where(lane < 2 * size, hi, value - hi).astype(bf16)

    lane = iota((16, 192), 1)
    sub = iota((16, 192), 0)
    seg = lane & 63
    part = seg >> 4
    step = row_of_place(seg & 15) - (sub & 7)
    tap_masks = []
    for i in range(3):
        for j in range(3):
            tap_masks.append((part == j) & (step == 2 * (i - 1)))
    bias_mask = seg == 48
    first = sub < 8

    def paint_pair(c, carry):
        value = jnp.where(bias_mask, jnp.where(first, bias[2 * c], bias[2 * c + 1]), 0.0)
        for tap in range(9):
            pair = jnp.where(first, weight[2 * c, tap], weight[2 * c + 1, tap])
            value = jnp.where(tap_masks[tap], pair, value)
        paint_lhs[pl.ds(pl.multiple_of(c * 16, 16), 16), :] = pack(value, lane, 64)
        return carry

    lax.fori_loop(0, channels // 2, paint_pair, 0)
    one_row = jnp.where(iota((16, block), 0) == 0, 1.0, 0.0).astype(f32)

    lane = iota((16, 240), 1)
    sub = iota((16, 240), 0)
    seg = jnp.where(lane >= 160, lane - 160, jnp.where(lane >= 80, lane - 80, lane))
    part = seg >> 4
    step = row_of_place(seg & 15) - jnp.where(sub < 8, sub, jnp.where(sub == 8, -1, 8))
    value = jnp.zeros((16, 240), f32)
    for a in range(5):
        for b in range(5):
            value = jnp.where((part == b) & (step == a - 2) & (sub < 10), short[a, b], value)
    short_lhs[...] = pack(value, lane, 80)

    spread[...] = ((iota((128, block), 1) >> 2) == iota((128, block), 0)).astype(f32).astype(bf16)
    pool = ((iota((block, 128), 0) >> 2) == iota((block, 128), 1)).astype(f32).astype(bf16)
    col_scale = cols / 16.0

    def col_rows(i, carry):
        gap = iota((64, coarse_cols), 0) + i * 64 - iota((64, coarse_cols), 1)
        hi, lo = split(jnp.exp(-jnp.abs(gap.astype(f32)) / col_scale))
        at = pl.ds(pl.multiple_of(i * 64, 64), 64)
        col_hi[at, :] = hi
        col_lo[at, :] = lo
        return carry

    lax.fori_loop(0, coarse_cols // 64, col_rows, 0)
    mass_own[:, :, pad : pad + cols] = density[...]
    edge_wait(mass_copy, 0)

    def paint(cb):
        sums = []
        for p in range(planes):
            parts = [mass_edge[p, :, at_window(cb)], mass_own[p, :, at_window(cb)]]
            stacked = []
            for j in range(3):
                stacked += [shifted(x, 2 * (j - 1)) for x in parts]
            stacked.append(one_row)
            hi, lo = split(jnp.concatenate(stacked, axis=0))
            pre = dot(paint_lhs[...], jnp.concatenate([hi, lo, hi], axis=0))
            total = jnp.zeros((rows, block), f32)
            for c in range(channels):
                total += mix[c] * jnp.tanh(pre[rows * c : rows * c + rows])
            conv_own[p, :, at_padded(cb)] = total
            sums.append(jnp.sum(total[0:4], axis=0, keepdims=True))
            sums.append(jnp.sum(total[4:8], axis=0, keepdims=True))
        sums += [jnp.zeros((1, block), f32)] * (8 - 2 * planes)
        hi, lo = split(jnp.concatenate(sums, axis=0) * (1.0 / 16.0))
        coarse = dot(hi, pool) + dot(lo, pool)
        gathered[t, :, pl.ds(pl.multiple_of(cb * 128, 128), 128)] = coarse

    def short_copy(cb, to):
        return pltpu.make_async_remote_copy(
            src_ref=shorts.at[g, :, :, at_block(cb)],
            dst_ref=shorts.at[g, :, :, at_block(cb)],
            send_sem=short_send.at[to, cb],
            recv_sem=short_recv.at[g, cb],
            device_id={"plane": to},
        )

    def long_copy(to):
        return pltpu.make_async_remote_copy(
            src_ref=longs.at[g],
            dst_ref=longs.at[g],
            send_sem=long_send.at[to],
            recv_sem=long_recv.at[g],
            device_id={"plane": to},
        )

    def short_block(cb):
        edges = []
        for p in range(planes):
            parts = [conv_edge[p, :, at_window(cb)], conv_own[p, :, at_window(cb)]]
            stacked = [shifted(x, b - 2) for b in range(5) for x in parts]
            hi, lo = split(jnp.concatenate(stacked, axis=0))
            value = dot(short_lhs[...], jnp.concatenate([hi, lo, hi], axis=0))
            shorts[g, p, :, at_block(cb)] = value[0:8]
            edges.append(value[8:10])
        edges += [jnp.zeros((8 - 2 * planes, block), f32)]
        shorts[g, planes, :, at_block(cb)] = jnp.concatenate(edges, axis=0)

        def short_start(to, carry):
            short_copy(cb, to).start()
            return carry

        lax.fori_loop(g + 1, groups, short_start, 0)

    def coarse_copy(j):
        return pltpu.make_async_remote_copy(
            src_ref=gathered.at[t],
            dst_ref=gathered.at[t],
            send_sem=coarse_send.at[j],
            recv_sem=coarse_recv.at[t],
            device_id={"tile": lax.rem(t + j, tiles)},
        )

    def coarse_start(j, carry):
        coarse_copy(j).start()
        return carry

    def paint_step(cb, carry):
        @pl.when(cb + 1 < blocks)
        def _():
            edge_wait(mass_copy, cb + 1)

        paint(cb)

        @pl.when(cb + 1 < blocks)
        def _():
            edge_start(conv_copy, cb)

        @pl.when(cb == 2)
        def _():
            edge_wait(conv_copy, 0)

        @pl.when(cb > 1)
        def _():
            edge_wait(conv_copy, cb - 1)
            short_block(cb - 2)

        return carry

    lax.fori_loop(0, blocks, paint_step, 0)
    lax.fori_loop(1, tiles, coarse_start, 0)
    edge_start(conv_copy, blocks - 1)
    short_rest = max(blocks - 2, 0)

    def short_step(cb, carry):
        @pl.when(cb + 1 < blocks)
        def _():
            edge_wait(conv_copy, cb + 1)

        short_block(cb)
        return carry

    lax.fori_loop(short_rest, blocks, short_step, 0)

    def coarse_wait(j, carry):
        source = lax.rem(t + j, tiles)
        pltpu.make_async_remote_copy(
            src_ref=gathered.at[source],
            dst_ref=gathered.at[source],
            send_sem=coarse_send.at[j],
            recv_sem=coarse_recv.at[source],
            device_id={"tile": source},
        ).wait_recv()
        return carry

    row_scale = tiles * rows / 16.0
    long_gain = 1.0 / math.sqrt(row_scale * col_scale)
    m = iota((16, tiles * 8), 0)
    n = iota((16, tiles * 8), 1)
    gap = (2 * t - 1 + (m & 3)) - (2 * (n >> 3) + (n & 1))
    near = jnp.exp(-jnp.abs(gap.astype(f32)) / row_scale) * long_gain
    row_kernel = jnp.where((m >> 2) == ((n & 7) >> 1), near, 0.0)
    row_hi, row_lo = split(row_kernel)
    row_lhs = jnp.concatenate([row_hi, row_hi, row_lo], axis=1)
    lax.fori_loop(1, tiles, coarse_wait, 0)
    hi, lo = split(gathered[...].reshape(tiles * 8, coarse_cols))
    hi, lo = split(dot(row_lhs, jnp.concatenate([hi, lo, hi], axis=0)))
    both = dot(jnp.concatenate([hi, lo], axis=0), col_hi[...])
    longs[g] = both[0:16] + both[16:32] + dot(hi, col_lo[...])

    def long_start(to, carry):
        long_copy(to).start()
        return carry

    lax.fori_loop(g + 1, groups, long_start, 0)

    for entry in range(4):
        for p in (planes - 2, planes - 1):
            out[entry, p] = jnp.full((rows, cols), 1.0 if entry in (0, 3) else 0.0, f32)
    row_at = iota((rows, cols), 0)
    col_at = iota((rows, cols), 1)
    low_gain = jnp.where(t > 0, 1.0, 0.0)
    high_gain = jnp.where(t < tiles - 1, 1.0, 0.0)
    slot_total = 2.0 * slots
    wide = cols // 128

    def next_col(x):
        return jnp.where(col_at == cols - 1, 0.0, pltpu.roll(x, cols - 1, 1))

    def last_col(x):
        return jnp.where(col_at == 0, 0.0, pltpu.roll(x, 1, 1))

    def lens(gi, carry):
        @pl.when(gi < g)
        def _():
            def short_wait(cb, carry):
                at = pl.ds(pl.multiple_of(cb * block, block), block)
                pltpu.make_async_remote_copy(
                    src_ref=shorts.at[gi, :, :, at],
                    dst_ref=shorts.at[gi, :, :, at],
                    send_sem=short_send.at[gi, cb],
                    recv_sem=short_recv.at[gi, cb],
                    device_id={"plane": gi},
                ).wait_recv()
                return carry

            lax.fori_loop(0, blocks, short_wait, 0)
            pltpu.make_async_remote_copy(
                src_ref=longs.at[gi],
                dst_ref=longs.at[gi],
                send_sem=long_send.at[gi],
                recv_sem=long_recv.at[gi],
                device_id={"plane": gi},
            ).wait_recv()

        hi, lo = split(longs[gi])
        pieces = coarse_cols // 128
        stacked = [x[:, 128 * b : 128 * b + 128] for x in (hi, lo) for b in range(pieces)]
        spread_out = dot(jnp.concatenate(stacked, axis=0), spread[...])
        upper = [
            spread_out[16 * b : 16 * b + 16]
            + spread_out[16 * (pieces + b) : 16 * (pieces + b) + 16]
            for b in range(pieces)
        ]
        long_wide = jnp.concatenate(upper, axis=1)
        edges = shorts[gi, planes]
        for p in range(planes):
            k = gi * planes + p

            def distance(index):
                value = jnp.full((8, 128), slot[index], jnp.int32)
                return (value.astype(f32) + 1.0) / slot_total

            here = distance(k)
            before = jnp.where(k > 0, distance(jnp.maximum(k - 1, 0)), 0.0)
            after = jnp.where(
                k < slots - 1,
                distance(jnp.minimum(k + 1, slots - 1)),
                (slot_total + 1.0) / slot_total,
            )
            mixing = before * (after - here) / (here * (after - before))
            bending = lens_gain * (after - here) / after
            mixing = jnp.concatenate([mixing] * wide, axis=1)
            bending = jnp.concatenate([bending] * wide, axis=1)
            center = shorts[gi, p] + jnp.where(
                row_at < 4, long_wide[4 * p + 1 : 4 * p + 2], long_wide[4 * p + 2 : 4 * p + 3]
            )
            top = (edges[2 * p : 2 * p + 1] + long_wide[4 * p : 4 * p + 1]) * low_gain
            bottom = (
                edges[2 * p + 1 : 2 * p + 2] + long_wide[4 * p + 3 : 4 * p + 4]
            ) * high_gain
            up = jnp.where(row_at == 0, top, pltpu.roll(center, 1, 0))
            down = jnp.where(row_at == rows - 1, bottom, pltpu.roll(center, rows - 1, 0))
            u11 = (down - 2.0 * center + up) * bending
            u22 = (next_col(center) - 2.0 * center + last_col(center)) * bending
            slope = down - up
            u12 = (next_col(slope) - last_col(slope)) * (0.25 * bending)
            old = [out[e, (p - 2) % planes] for e in range(4)]
            new = [out[e, (p - 1) % planes] for e in range(4)]
            bent = [
                u11 * new[0] + u12 * new[2],
                u11 * new[1] + u12 * new[3],
                u12 * new[0] + u22 * new[2],
                u12 * new[1] + u22 * new[3],
            ]
            for e in range(4):
                out[e, p] = (1.0 - mixing) * old[e] + mixing * new[e] - bent[e]
        return carry

    lax.fori_loop(0, g + 1, lens, 0)

    def block_sent(cb, carry):
        edge_sent(mass_copy, cb)
        edge_sent(conv_copy, cb)
        return carry

    lax.fori_loop(0, blocks, block_sent, 0)

    def coarse_sent(j, carry):
        coarse_copy(j).wait_send()
        return carry

    lax.fori_loop(1, tiles, coarse_sent, 0)

    def later_sent(to, carry):
        def short_sent(cb, inner):
            short_copy(cb, to).wait_send()
            return inner

        lax.fori_loop(0, blocks, short_sent, 0)
        long_copy(to).wait_send()
        return carry

    lax.fori_loop(g + 1, groups, later_sent, 0)


def solution(mesh):
    tiles, groups = mesh.shape["tile"], mesh.shape["plane"]

    def body(density, plane_slot, paint_weight, paint_bias, mix_weight, short_kernel):
        planes, rows, cols = density.shape
        channels = paint_weight.shape[0]
        coarse_cols = cols // 4
        blocks = cols // block
        vmem = pl.BlockSpec(memory_space=pltpu.VMEM)
        smem = pl.BlockSpec(memory_space=pltpu.SMEM)
        wide = cols + 2 * pad
        dma = pltpu.SemaphoreType.DMA
        map_shape = pltpu.VMEM((planes, rows, wide), f32)
        return pl.pallas_call(
            functools.partial(kernel, tiles, groups),
            out_shape=jax.ShapeDtypeStruct((4, planes, rows, cols), f32),
            in_specs=[vmem] + [smem] * 5,
            out_specs=vmem,
            scratch_shapes=[
                map_shape,
                map_shape,
                map_shape,
                map_shape,
                pltpu.VMEM((8 * channels, 192), bf16),
                pltpu.VMEM((16, 240), bf16),
                pltpu.VMEM((coarse_cols, coarse_cols), bf16),
                pltpu.VMEM((coarse_cols, coarse_cols), bf16),
                pltpu.VMEM((128, block), bf16),
                pltpu.VMEM((tiles, 8, coarse_cols), f32),
                pltpu.VMEM((groups, planes + 1, rows, cols), f32),
                pltpu.VMEM((groups, 16, coarse_cols), f32),
                dma((2, blocks)),
                dma((2, blocks)),
                dma((2, blocks)),
                dma((2, blocks)),
                dma((tiles,)),
                dma((tiles,)),
                dma((groups, blocks)),
                dma((groups, blocks)),
                dma((groups,)),
                dma((groups,)),
            ],
            compiler_params=pltpu.CompilerParams(
                collective_id=0, has_side_effects=True, vmem_limit_bytes=48 * 1024 * 1024
            ),
        )(density, plane_slot, paint_weight, paint_bias, mix_weight, short_kernel)

    placed = (P("plane", "tile", None), P(), P(), P(), P(), P())
    return jax.shard_map(
        body, mesh=mesh, in_specs=placed, out_specs=P(None, "plane", "tile", None), check_vma=False
    )
```

```python
import functools
import math

import jax
import jax.numpy as jnp
from jax import lax
from jax.experimental import pallas as pl
from jax.experimental.pallas import tpu as pltpu
from jax.sharding import PartitionSpec as P

lens_gain = 0.25
pad = 128
block = 256
span = 512
f32 = jnp.float32
bf16 = jnp.bfloat16


def split(x):
    hi = x.astype(bf16)
    return hi, (x - hi.astype(f32)).astype(bf16)


def iota(shape, axis):
    return lax.broadcasted_iota(jnp.int32, shape, axis)


def dot(a, b):
    return jnp.dot(a, b, preferred_element_type=f32)


def kernel(
    tiles, groups, density, slot, weight, bias, mix, short, out,
    mass_own, mass_edge, conv_own, conv_edge, paint_lhs, short_lhs, col_hi, col_lo, spread,
    gathered, shorts, longs, row_sums, field_own, field_now,
    mass_send, mass_recv, conv_send, conv_recv, coarse_send, coarse_recv,
    short_send, short_recv, long_send, long_recv,
):
    planes, rows, cols = density.shape
    channels = weight.shape[0]
    slots = slot.shape[0]
    blocks = cols // block
    coarse_cols = cols // 4
    half = rows // 2
    t = lax.axis_index("tile")
    g = lax.axis_index("plane")
    has_low = t > 0
    has_high = t < tiles - 1

    def at_block(cb):
        return pl.ds(pl.multiple_of(cb * block, block), block)

    def at_padded(cb):
        return pl.ds(pl.multiple_of(cb * block + pad, pad), block)

    def at_window(cb):
        return pl.ds(pl.multiple_of(cb * block, block), block + 2 * pad)

    def shifted(x, by):
        moved = x if by == 0 else pltpu.roll(x, (-by) % (block + 2 * pad), 1)
        return moved[:, pad : pad + block]

    barrier = pltpu.get_barrier_semaphore()

    def greet_tile(j, carry):
        pl.semaphore_signal(barrier, inc=1, device_id={"tile": lax.rem(t + j, tiles)})
        return carry

    def greet_plane(j, carry):
        pl.semaphore_signal(barrier, inc=1, device_id={"plane": lax.rem(g + j, groups)})
        return carry

    lax.fori_loop(1, tiles, greet_tile, 0)
    lax.fori_loop(1, groups, greet_plane, 0)
    pl.semaphore_wait(barrier, tiles + groups - 2)

    def edge_copy(source, source_at, target, send, recv, side, cb):
        take = pl.ds(half, half) if side == 0 else pl.ds(0, half)
        give = pl.ds(0, half) if side == 0 else pl.ds(half, half)
        return pltpu.make_async_remote_copy(
            src_ref=source.at[:, take, source_at(cb)],
            dst_ref=target.at[:, give, at_padded(cb)],
            send_sem=send.at[side, cb],
            recv_sem=recv.at[side, cb],
            device_id={"tile": lax.rem(t + (1 if side == 0 else tiles - 1), tiles)},
        )

    def mass_copy(side, cb):
        return edge_copy(density, at_block, mass_edge, mass_send, mass_recv, side, cb)

    def conv_copy(side, cb):
        return edge_copy(conv_own, at_padded, conv_edge, conv_send, conv_recv, side, cb)

    def edge_start(copy, cb):
        @pl.when(has_high)
        def _():
            copy(0, cb).start()

        @pl.when(has_low)
        def _():
            copy(1, cb).start()

    def edge_wait(copy, cb):
        @pl.when(has_low)
        def _():
            copy(0, cb).wait_recv()

        @pl.when(has_high)
        def _():
            copy(1, cb).wait_recv()

    def edge_sent(copy, cb):
        @pl.when(has_high)
        def _():
            copy(0, cb).wait_send()

        @pl.when(has_low)
        def _():
            copy(1, cb).wait_send()

    def mass_start(cb, carry):
        edge_start(mass_copy, cb)
        return carry

    lax.fori_loop(0, blocks, mass_start, 0)

    for buffer in (mass_own, mass_edge, conv_own, conv_edge):
        buffer[:, :, 0:pad] = jnp.zeros((planes, rows, pad), f32)
        buffer[:, :, pad + cols :] = jnp.zeros((planes, rows, pad), f32)
    for buffer in (mass_edge, conv_edge):

        @pl.when(jnp.logical_not(has_low))
        def _():
            buffer[:, 0:half, pad : pad + cols] = jnp.zeros((planes, half, cols), f32)

        @pl.when(jnp.logical_not(has_high))
        def _():
            buffer[:, half:rows, pad : pad + cols] = jnp.zeros((planes, half, cols), f32)

    def row_of_place(place):
        return jnp.where(place < half, place - half, jnp.where(place < rows, place + half, place - rows))

    def pack(value, lane, size):
        hi = value.astype(bf16).astype(f32)
        return jnp.where(lane < 2 * size, hi, value - hi).astype(bf16)

    lane = iota((16, 192), 1)
    sub = iota((16, 192), 0)
    seg = lane & 63
    part = seg >> 4
    step = row_of_place(seg & 15) - (sub & 7)
    tap_masks = []
    for i in range(3):
        for j in range(3):
            tap_masks.append((part == j) & (step == 2 * (i - 1)))
    bias_mask = seg == 48
    first = sub < 8

    def paint_pair(c, carry):
        value = jnp.where(bias_mask, jnp.where(first, bias[2 * c], bias[2 * c + 1]), 0.0)
        for tap in range(9):
            pair = jnp.where(first, weight[2 * c, tap], weight[2 * c + 1, tap])
            value = jnp.where(tap_masks[tap], pair, value)
        paint_lhs[pl.ds(pl.multiple_of(c * 16, 16), 16), :] = pack(value, lane, 64)
        return carry

    lax.fori_loop(0, channels // 2, paint_pair, 0)
    one_row = jnp.where(iota((16, block), 0) == 0, 1.0, 0.0).astype(f32)

    lane = iota((16, 240), 1)
    sub = iota((16, 240), 0)
    seg = jnp.where(lane >= 160, lane - 160, jnp.where(lane >= 80, lane - 80, lane))
    part = seg >> 4
    step = row_of_place(seg & 15) - jnp.where(sub < 8, sub, jnp.where(sub == 8, -1, 8))
    value = jnp.zeros((16, 240), f32)
    for a in range(5):
        for b in range(5):
            value = jnp.where((part == b) & (step == a - 2) & (sub < 10), short[a, b], value)
    short_lhs[...] = pack(value, lane, 80)

    spread[...] = ((iota((128, span), 1) >> 2) == iota((128, span), 0)).astype(f32).astype(bf16)
    pool = ((iota((span, 128), 0) >> 2) == iota((span, 128), 1)).astype(f32).astype(bf16)
    col_scale = cols / 16.0

    def col_rows(i, carry):
        gap = iota((64, coarse_cols), 0) + i * 64 - iota((64, coarse_cols), 1)
        hi, lo = split(jnp.exp(-jnp.abs(gap.astype(f32)) / col_scale))
        at = pl.ds(pl.multiple_of(i * 64, 64), 64)
        col_hi[at, :] = hi
        col_lo[at, :] = lo
        return carry

    lax.fori_loop(0, coarse_cols // 64, col_rows, 0)
    mass_own[:, :, pad : pad + cols] = density[...]
    edge_wait(mass_copy, 0)

    def paint(cb):
        sums = []
        for p in range(planes):
            parts = [mass_edge[p, :, at_window(cb)], mass_own[p, :, at_window(cb)]]
            stacked = []
            for j in range(3):
                stacked += [shifted(x, 2 * (j - 1)) for x in parts]
            stacked.append(one_row)
            hi, lo = split(jnp.concatenate(stacked, axis=0))
            pre = dot(paint_lhs[...], jnp.concatenate([hi, lo, hi], axis=0))
            total = jnp.zeros((rows, block), f32)
            for c in range(channels):
                total += mix[c] * jnp.tanh(pre[rows * c : rows * c + rows])
            conv_own[p, :, at_padded(cb)] = total
            sums.append(jnp.sum(total[0:4], axis=0, keepdims=True))
            sums.append(jnp.sum(total[4:8], axis=0, keepdims=True))
        sums += [jnp.zeros((1, block), f32)] * (8 - 2 * planes)
        row_sums[:, at_block(cb)] = jnp.concatenate(sums, axis=0) * (1.0 / 16.0)

    def pool_columns():
        count = cols // span
        sums = row_sums[...]
        pieces = [sums[:, span * b : span * b + span] for b in range(count)]
        hi, lo = split(jnp.concatenate(pieces, axis=0))
        pooled = dot(jnp.concatenate([hi, lo], axis=0), pool)
        for b in range(count):
            gathered[t, :, 128 * b : 128 * b + 128] = (
                pooled[8 * b : 8 * b + 8] + pooled[8 * (count + b) : 8 * (count + b) + 8]
            )

    def short_copy(cb, to):
        return pltpu.make_async_remote_copy(
            src_ref=shorts.at[g, :, :, at_block(cb)],
            dst_ref=shorts.at[g, :, :, at_block(cb)],
            send_sem=short_send.at[to, cb],
            recv_sem=short_recv.at[g, cb],
            device_id={"plane": to},
        )

    def long_copy(to):
        return pltpu.make_async_remote_copy(
            src_ref=longs.at[g],
            dst_ref=longs.at[g],
            send_sem=long_send.at[to],
            recv_sem=long_recv.at[g],
            device_id={"plane": to},
        )

    def short_block(cb):
        edges = []
        for p in range(planes):
            parts = [conv_edge[p, :, at_window(cb)], conv_own[p, :, at_window(cb)]]
            stacked = [shifted(x, b - 2) for b in range(5) for x in parts]
            hi, lo = split(jnp.concatenate(stacked, axis=0))
            value = dot(short_lhs[...], jnp.concatenate([hi, lo, hi], axis=0))
            shorts[g, p, :, at_block(cb)] = value[0:8]
            edges.append(value[8:10])
        edges += [jnp.zeros((8 - 2 * planes, block), f32)]
        shorts[g, planes, :, at_block(cb)] = jnp.concatenate(edges, axis=0)

        def short_start(to, carry):
            short_copy(cb, to).start()
            return carry

        lax.fori_loop(g + 1, groups, short_start, 0)

    def coarse_copy(j):
        return pltpu.make_async_remote_copy(
            src_ref=gathered.at[t],
            dst_ref=gathered.at[t],
            send_sem=coarse_send.at[j],
            recv_sem=coarse_recv.at[t],
            device_id={"tile": lax.rem(t + j, tiles)},
        )

    def coarse_start(j, carry):
        coarse_copy(j).start()
        return carry

    def paint_step(cb, carry):
        @pl.when(cb + 1 < blocks)
        def _():
            edge_wait(mass_copy, cb + 1)

        paint(cb)

        @pl.when(cb + 1 < blocks)
        def _():
            edge_start(conv_copy, cb)

        @pl.when(cb == 2)
        def _():
            edge_wait(conv_copy, 0)

        @pl.when(cb > 1)
        def _():
            edge_wait(conv_copy, cb - 1)
            short_block(cb - 2)

        return carry

    lax.fori_loop(0, blocks, paint_step, 0)
    pool_columns()
    lax.fori_loop(1, tiles, coarse_start, 0)
    edge_start(conv_copy, blocks - 1)
    short_rest = max(blocks - 2, 0)

    def short_step(cb, carry):
        @pl.when(cb + 1 < blocks)
        def _():
            edge_wait(conv_copy, cb + 1)

        short_block(cb)
        return carry

    lax.fori_loop(short_rest, blocks, short_step, 0)

    def coarse_wait(j, carry):
        source = lax.rem(t + j, tiles)
        pltpu.make_async_remote_copy(
            src_ref=gathered.at[source],
            dst_ref=gathered.at[source],
            send_sem=coarse_send.at[j],
            recv_sem=coarse_recv.at[source],
            device_id={"tile": source},
        ).wait_recv()
        return carry

    row_scale = tiles * rows / 16.0
    long_gain = 1.0 / math.sqrt(row_scale * col_scale)
    m = iota((16, tiles * 8), 0)
    n = iota((16, tiles * 8), 1)
    gap = (2 * t - 1 + (m & 3)) - (2 * (n >> 3) + (n & 1))
    near = jnp.exp(-jnp.abs(gap.astype(f32)) / row_scale) * long_gain
    row_kernel = jnp.where((m >> 2) == ((n & 7) >> 1), near, 0.0)
    row_hi, row_lo = split(row_kernel)
    row_lhs = jnp.concatenate([row_hi, row_hi, row_lo], axis=1)
    lax.fori_loop(1, tiles, coarse_wait, 0)
    hi, lo = split(gathered[...].reshape(tiles * 8, coarse_cols))
    hi, lo = split(dot(row_lhs, jnp.concatenate([hi, lo, hi], axis=0)))
    both = dot(jnp.concatenate([hi, lo], axis=0), col_hi[...])
    longs[g] = both[0:16] + both[16:32] + dot(hi, col_lo[...])

    def long_start(to, carry):
        long_copy(to).start()
        return carry

    lax.fori_loop(g + 1, groups, long_start, 0)

    for entry in range(4):
        for p in (planes - 2, planes - 1):
            out[entry, p] = jnp.full((rows, cols), 1.0 if entry in (0, 3) else 0.0, f32)
    row_at = iota((rows, cols), 0)
    col_at = iota((rows, cols), 1)
    low_gain = jnp.where(t > 0, 1.0, 0.0)
    high_gain = jnp.where(t < tiles - 1, 1.0, 0.0)
    slot_total = 2.0 * slots
    wide = cols // 128

    def next_col(x):
        return jnp.where(col_at == cols - 1, 0.0, pltpu.roll(x, cols - 1, 1))

    def last_col(x):
        return jnp.where(col_at == 0, 0.0, pltpu.roll(x, 1, 1))

    def hessian(gi, field):
        hi, lo = split(longs[gi])
        pieces = coarse_cols // 128
        stacked = [x[:, 128 * b : 128 * b + 128] for x in (hi, lo) for b in range(pieces)]
        spread_out = dot(jnp.concatenate(stacked, axis=0), spread[...])
        upper = [
            spread_out[16 * b : 16 * b + 16]
            + spread_out[16 * (pieces + b) : 16 * (pieces + b) + 16]
            for b in range(pieces)
        ]
        long_wide = jnp.concatenate(upper, axis=1)
        edges = shorts[gi, planes]
        for p in range(planes):
            center = shorts[gi, p] + jnp.where(
                row_at < 4, long_wide[4 * p + 1 : 4 * p + 2], long_wide[4 * p + 2 : 4 * p + 3]
            )
            top = (edges[2 * p : 2 * p + 1] + long_wide[4 * p : 4 * p + 1]) * low_gain
            bottom = (
                edges[2 * p + 1 : 2 * p + 2] + long_wide[4 * p + 3 : 4 * p + 4]
            ) * high_gain
            up = jnp.where(row_at == 0, top, pltpu.roll(center, 1, 0))
            down = jnp.where(row_at == rows - 1, bottom, pltpu.roll(center, rows - 1, 0))
            field[0, p] = (down - 2.0 * center + up)
            field[1, p] = (next_col(center) - 2.0 * center + last_col(center))
            slope = down - up
            field[2, p] = (next_col(slope) - last_col(slope)) * 0.25

    def advance(gi, field):
        for p in range(planes):
            k = gi * planes + p

            def distance(index):
                value = jnp.full((8, 128), slot[index], jnp.int32)
                return (value.astype(f32) + 1.0) / slot_total

            here = distance(k)
            before = jnp.where(k > 0, distance(jnp.maximum(k - 1, 0)), 0.0)
            after = jnp.where(
                k < slots - 1,
                distance(jnp.minimum(k + 1, slots - 1)),
                (slot_total + 1.0) / slot_total,
            )
            mixing = before * (after - here) / (here * (after - before))
            bending = lens_gain * (after - here) / after
            mixing = jnp.concatenate([mixing] * wide, axis=1)
            bending = jnp.concatenate([bending] * wide, axis=1)
            old = [out[e, (p - 2) % planes] for e in range(4)]
            new = [out[e, (p - 1) % planes] for e in range(4)]
            u11, u22, u12 = [field[i, p] * bending for i in range(3)]
            bent = [
                u11 * new[0] + u12 * new[2],
                u11 * new[1] + u12 * new[3],
                u12 * new[0] + u22 * new[2],
                u12 * new[1] + u22 * new[3],
            ]
            for e in range(4):
                out[e, p] = (1.0 - mixing) * old[e] + mixing * new[e] - bent[e]

    def lens(gi, carry):
        def short_wait(cb, carry):
            at = pl.ds(pl.multiple_of(cb * block, block), block)
            pltpu.make_async_remote_copy(
                src_ref=shorts.at[gi, :, :, at],
                dst_ref=shorts.at[gi, :, :, at],
                send_sem=short_send.at[gi, cb],
                recv_sem=short_recv.at[gi, cb],
                device_id={"plane": gi},
            ).wait_recv()
            return carry

        lax.fori_loop(0, blocks, short_wait, 0)
        pltpu.make_async_remote_copy(
            src_ref=longs.at[gi],
            dst_ref=longs.at[gi],
            send_sem=long_send.at[gi],
            recv_sem=long_recv.at[gi],
            device_id={"plane": gi},
        ).wait_recv()

        hessian(gi, field_now)
        advance(gi, field_now)
        return carry

    hessian(g, field_own)
    lax.fori_loop(0, g, lens, 0)
    advance(g, field_own)

    def block_sent(cb, carry):
        edge_sent(mass_copy, cb)
        edge_sent(conv_copy, cb)
        return carry

    lax.fori_loop(0, blocks, block_sent, 0)

    def coarse_sent(j, carry):
        coarse_copy(j).wait_send()
        return carry

    lax.fori_loop(1, tiles, coarse_sent, 0)

    def later_sent(to, carry):
        def short_sent(cb, inner):
            short_copy(cb, to).wait_send()
            return inner

        lax.fori_loop(0, blocks, short_sent, 0)
        long_copy(to).wait_send()
        return carry

    lax.fori_loop(g + 1, groups, later_sent, 0)


def solution(mesh):
    tiles, groups = mesh.shape["tile"], mesh.shape["plane"]

    def body(density, plane_slot, paint_weight, paint_bias, mix_weight, short_kernel):
        planes, rows, cols = density.shape
        channels = paint_weight.shape[0]
        coarse_cols = cols // 4
        blocks = cols // block
        vmem = pl.BlockSpec(memory_space=pltpu.VMEM)
        smem = pl.BlockSpec(memory_space=pltpu.SMEM)
        wide = cols + 2 * pad
        dma = pltpu.SemaphoreType.DMA
        map_shape = pltpu.VMEM((planes, rows, wide), f32)
        return pl.pallas_call(
            functools.partial(kernel, tiles, groups),
            out_shape=jax.ShapeDtypeStruct((4, planes, rows, cols), f32),
            in_specs=[vmem] + [smem] * 5,
            out_specs=vmem,
            scratch_shapes=[
                map_shape,
                map_shape,
                map_shape,
                map_shape,
                pltpu.VMEM((8 * channels, 192), bf16),
                pltpu.VMEM((16, 240), bf16),
                pltpu.VMEM((coarse_cols, coarse_cols), bf16),
                pltpu.VMEM((coarse_cols, coarse_cols), bf16),
                pltpu.VMEM((128, span), bf16),
                pltpu.VMEM((tiles, 8, coarse_cols), f32),
                pltpu.VMEM((groups, planes + 1, rows, cols), f32),
                pltpu.VMEM((groups, 16, coarse_cols), f32),
                pltpu.VMEM((8, cols), f32),
                pltpu.VMEM((3, planes, rows, cols), f32),
                pltpu.VMEM((3, planes, rows, cols), f32),
                dma((2, blocks)),
                dma((2, blocks)),
                dma((2, blocks)),
                dma((2, blocks)),
                dma((tiles,)),
                dma((tiles,)),
                dma((groups, blocks)),
                dma((groups, blocks)),
                dma((groups,)),
                dma((groups,)),
            ],
            compiler_params=pltpu.CompilerParams(
                collective_id=0, has_side_effects=True, vmem_limit_bytes=48 * 1024 * 1024
            ),
        )(density, plane_slot, paint_weight, paint_bias, mix_weight, short_kernel)

    placed = (P("plane", "tile", None), P(), P(), P(), P(), P())
    return jax.shard_map(
        body, mesh=mesh, in_specs=placed, out_specs=P(None, "plane", "tile", None), check_vma=False
    )
```

```python
import functools
import math

import jax
import jax.numpy as jnp
from jax import lax
from jax.experimental import pallas as pl
from jax.experimental.pallas import tpu as pltpu
from jax.sharding import PartitionSpec as P

lens_gain = 0.25
pad = 128
block = 512
span = 512
f32 = jnp.float32
bf16 = jnp.bfloat16


def split(x):
    hi = x.astype(bf16)
    return hi, (x - hi.astype(f32)).astype(bf16)


def iota(shape, axis):
    return lax.broadcasted_iota(jnp.int32, shape, axis)


def dot(a, b):
    return jnp.dot(a, b, preferred_element_type=f32)


def kernel(
    tiles, groups, density, slot, weight, bias, mix, short, out,
    mass_own, mass_edge, conv_own, conv_edge, paint_lhs, short_lhs, col_hi, col_lo, spread,
    gathered, shorts, longs, row_sums, field_own, field_now,
    mass_send, mass_recv, conv_send, conv_recv, coarse_send, coarse_recv,
    short_send, short_recv, long_send, long_recv,
):
    planes, rows, cols = density.shape
    channels = weight.shape[0]
    slots = slot.shape[0]
    blocks = cols // block
    coarse_cols = cols // 4
    half = rows // 2
    t = lax.axis_index("tile")
    g = lax.axis_index("plane")
    has_low = t > 0
    has_high = t < tiles - 1

    def place_of(start, size):
        return pl.ds(start if isinstance(start, int) else pl.multiple_of(start, pad), size)

    def at_block(cb):
        return place_of(cb * block, block)

    def at_padded(cb):
        return place_of(cb * block + pad, block)

    def at_window(cb):
        return place_of(cb * block, block + 2 * pad)

    def shifted(x, by):
        moved = x if by == 0 else pltpu.roll(x, (-by) % (block + 2 * pad), 1)
        return moved[:, pad : pad + block]

    barrier = pltpu.get_barrier_semaphore()

    def greet_tile(j, carry):
        pl.semaphore_signal(barrier, inc=1, device_id={"tile": lax.rem(t + j, tiles)})
        return carry

    def greet_plane(j, carry):
        pl.semaphore_signal(barrier, inc=1, device_id={"plane": lax.rem(g + j, groups)})
        return carry

    lax.fori_loop(1, tiles, greet_tile, 0)
    lax.fori_loop(1, groups, greet_plane, 0)
    pl.semaphore_wait(barrier, tiles + groups - 2)

    def edge_copy(source, source_at, target, send, recv, side, cb):
        take = pl.ds(half, half) if side == 0 else pl.ds(0, half)
        give = pl.ds(0, half) if side == 0 else pl.ds(half, half)
        return pltpu.make_async_remote_copy(
            src_ref=source.at[:, take, source_at(cb)],
            dst_ref=target.at[:, give, at_padded(cb)],
            send_sem=send.at[side, cb],
            recv_sem=recv.at[side, cb],
            device_id={"tile": lax.rem(t + (1 if side == 0 else tiles - 1), tiles)},
        )

    def mass_copy(side, cb):
        return edge_copy(density, at_block, mass_edge, mass_send, mass_recv, side, cb)

    def conv_copy(side, cb):
        return edge_copy(conv_own, at_padded, conv_edge, conv_send, conv_recv, side, cb)

    def edge_start(copy, cb):
        @pl.when(has_high)
        def _():
            copy(0, cb).start()

        @pl.when(has_low)
        def _():
            copy(1, cb).start()

    def edge_wait(copy, cb):
        @pl.when(has_low)
        def _():
            copy(0, cb).wait_recv()

        @pl.when(has_high)
        def _():
            copy(1, cb).wait_recv()

    def edge_sent(copy, cb):
        @pl.when(has_high)
        def _():
            copy(0, cb).wait_send()

        @pl.when(has_low)
        def _():
            copy(1, cb).wait_send()

    def mass_start(cb, carry):
        edge_start(mass_copy, cb)
        return carry

    lax.fori_loop(0, blocks, mass_start, 0)

    for buffer in (mass_own, mass_edge, conv_own, conv_edge):
        buffer[:, :, 0:pad] = jnp.zeros((planes, rows, pad), f32)
        buffer[:, :, pad + cols :] = jnp.zeros((planes, rows, pad), f32)
    for buffer in (mass_edge, conv_edge):

        @pl.when(jnp.logical_not(has_low))
        def _():
            buffer[:, 0:half, pad : pad + cols] = jnp.zeros((planes, half, cols), f32)

        @pl.when(jnp.logical_not(has_high))
        def _():
            buffer[:, half:rows, pad : pad + cols] = jnp.zeros((planes, half, cols), f32)

    def row_of_place(place):
        return jnp.where(place < half, place - half, jnp.where(place < rows, place + half, place - rows))

    def pack(value, lane, size):
        hi = value.astype(bf16).astype(f32)
        return jnp.where(lane < 2 * size, hi, value - hi).astype(bf16)

    lane = iota((16, 192), 1)
    sub = iota((16, 192), 0)
    seg = lane & 63
    part = seg >> 4
    step = row_of_place(seg & 15) - (sub & 7)
    tap_masks = []
    for i in range(3):
        for j in range(3):
            tap_masks.append((part == j) & (step == 2 * (i - 1)))
    bias_mask = seg == 48
    first = sub < 8

    def paint_pair(c, carry):
        value = jnp.where(bias_mask, jnp.where(first, bias[2 * c], bias[2 * c + 1]), 0.0)
        for tap in range(9):
            pair = jnp.where(first, weight[2 * c, tap], weight[2 * c + 1, tap])
            value = jnp.where(tap_masks[tap], pair, value)
        paint_lhs[pl.ds(pl.multiple_of(c * 16, 16), 16), :] = pack(value, lane, 64)
        return carry

    lax.fori_loop(0, channels // 2, paint_pair, 0)
    one_row = jnp.where(iota((16, block), 0) == 0, 1.0, 0.0).astype(f32)

    lane = iota((16, 240), 1)
    sub = iota((16, 240), 0)
    seg = jnp.where(lane >= 160, lane - 160, jnp.where(lane >= 80, lane - 80, lane))
    part = seg >> 4
    step = row_of_place(seg & 15) - jnp.where(sub < 8, sub, jnp.where(sub == 8, -1, 8))
    value = jnp.zeros((16, 240), f32)
    for a in range(5):
        for b in range(5):
            value = jnp.where((part == b) & (step == a - 2) & (sub < 10), short[a, b], value)
    short_lhs[...] = pack(value, lane, 80)

    spread[...] = ((iota((128, span), 1) >> 2) == iota((128, span), 0)).astype(f32).astype(bf16)
    pool = ((iota((span, 128), 0) >> 2) == iota((span, 128), 1)).astype(f32).astype(bf16)
    col_scale = cols / 16.0

    def col_rows(i, carry):
        gap = iota((64, coarse_cols), 0) + i * 64 - iota((64, coarse_cols), 1)
        hi, lo = split(jnp.exp(-jnp.abs(gap.astype(f32)) / col_scale))
        at = pl.ds(pl.multiple_of(i * 64, 64), 64)
        col_hi[at, :] = hi
        col_lo[at, :] = lo
        return carry

    lax.fori_loop(0, coarse_cols // 64, col_rows, 0)
    mass_own[:, :, pad : pad + cols] = density[...]
    for cb in range(blocks):
        edge_wait(mass_copy, cb)

    def paint(cb):
        sums = []
        for p in range(planes):
            parts = [mass_edge[p, :, at_window(cb)], mass_own[p, :, at_window(cb)]]
            stacked = []
            for j in range(3):
                stacked += [shifted(x, 2 * (j - 1)) for x in parts]
            stacked.append(one_row)
            hi, lo = split(jnp.concatenate(stacked, axis=0))
            pre = dot(paint_lhs[...], jnp.concatenate([hi, lo, hi], axis=0))
            total = jnp.zeros((rows, block), f32)
            for c in range(channels):
                total += mix[c] * jnp.tanh(pre[rows * c : rows * c + rows])
            conv_own[p, :, at_padded(cb)] = total
            sums.append(jnp.sum(total[0:4], axis=0, keepdims=True))
            sums.append(jnp.sum(total[4:8], axis=0, keepdims=True))
        sums += [jnp.zeros((1, block), f32)] * (8 - 2 * planes)
        row_sums[:, at_block(cb)] = jnp.concatenate(sums, axis=0) * (1.0 / 16.0)

    def pool_columns():
        count = cols // span
        sums = row_sums[...]
        pieces = [sums[:, span * b : span * b + span] for b in range(count)]
        hi, lo = split(jnp.concatenate(pieces, axis=0))
        pooled = dot(jnp.concatenate([hi, lo], axis=0), pool)
        for b in range(count):
            gathered[t, :, 128 * b : 128 * b + 128] = (
                pooled[8 * b : 8 * b + 8] + pooled[8 * (count + b) : 8 * (count + b) + 8]
            )

    def short_copy(cb, to):
        return pltpu.make_async_remote_copy(
            src_ref=shorts.at[g, :, :, at_block(cb)],
            dst_ref=shorts.at[g, :, :, at_block(cb)],
            send_sem=short_send.at[to, cb],
            recv_sem=short_recv.at[g, cb],
            device_id={"plane": to},
        )

    def long_copy(to):
        return pltpu.make_async_remote_copy(
            src_ref=longs.at[g],
            dst_ref=longs.at[g],
            send_sem=long_send.at[to],
            recv_sem=long_recv.at[g],
            device_id={"plane": to},
        )

    def short_block(cb):
        edges = []
        for p in range(planes):
            parts = [conv_edge[p, :, at_window(cb)], conv_own[p, :, at_window(cb)]]
            stacked = [shifted(x, b - 2) for b in range(5) for x in parts]
            hi, lo = split(jnp.concatenate(stacked, axis=0))
            value = dot(short_lhs[...], jnp.concatenate([hi, lo, hi], axis=0))
            shorts[g, p, :, at_block(cb)] = value[0:8]
            edges.append(value[8:10])
        edges += [jnp.zeros((8 - 2 * planes, block), f32)]
        shorts[g, planes, :, at_block(cb)] = jnp.concatenate(edges, axis=0)

        def short_start(to, carry):
            short_copy(cb, to).start()
            return carry

        lax.fori_loop(g + 1, groups, short_start, 0)

    def coarse_copy(j):
        return pltpu.make_async_remote_copy(
            src_ref=gathered.at[t],
            dst_ref=gathered.at[t],
            send_sem=coarse_send.at[j],
            recv_sem=coarse_recv.at[t],
            device_id={"tile": lax.rem(t + j, tiles)},
        )

    def coarse_start(j, carry):
        coarse_copy(j).start()
        return carry

    for cb in range(blocks):
        paint(cb)
        if cb + 1 < blocks:
            edge_start(conv_copy, cb)

    pool_columns()
    lax.fori_loop(1, tiles, coarse_start, 0)
    edge_start(conv_copy, blocks - 1)
    edge_wait(conv_copy, 0)
    for cb in range(blocks):
        if cb + 1 < blocks:
            edge_wait(conv_copy, cb + 1)
        short_block(cb)

    def coarse_wait(j, carry):
        source = lax.rem(t + j, tiles)
        pltpu.make_async_remote_copy(
            src_ref=gathered.at[source],
            dst_ref=gathered.at[source],
            send_sem=coarse_send.at[j],
            recv_sem=coarse_recv.at[source],
            device_id={"tile": source},
        ).wait_recv()
        return carry

    row_scale = tiles * rows / 16.0
    long_gain = 1.0 / math.sqrt(row_scale * col_scale)
    m = iota((16, tiles * 8), 0)
    n = iota((16, tiles * 8), 1)
    gap = (2 * t - 1 + (m & 3)) - (2 * (n >> 3) + (n & 1))
    near = jnp.exp(-jnp.abs(gap.astype(f32)) / row_scale) * long_gain
    row_kernel = jnp.where((m >> 2) == ((n & 7) >> 1), near, 0.0)
    row_hi, row_lo = split(row_kernel)
    row_lhs = jnp.concatenate([row_hi, row_hi, row_lo], axis=1)
    lax.fori_loop(1, tiles, coarse_wait, 0)
    hi, lo = split(gathered[...].reshape(tiles * 8, coarse_cols))
    hi, lo = split(dot(row_lhs, jnp.concatenate([hi, lo, hi], axis=0)))
    both = dot(jnp.concatenate([hi, lo], axis=0), col_hi[...])
    longs[g] = both[0:16] + both[16:32] + dot(hi, col_lo[...])

    def long_start(to, carry):
        long_copy(to).start()
        return carry

    lax.fori_loop(g + 1, groups, long_start, 0)

    for entry in range(4):
        for p in (planes - 2, planes - 1):
            out[entry, p] = jnp.full((rows, cols), 1.0 if entry in (0, 3) else 0.0, f32)
    row_at = iota((rows, cols), 0)
    col_at = iota((rows, cols), 1)
    low_gain = jnp.where(t > 0, 1.0, 0.0)
    high_gain = jnp.where(t < tiles - 1, 1.0, 0.0)
    slot_total = 2.0 * slots
    wide = cols // 128

    def next_col(x):
        return jnp.where(col_at == cols - 1, 0.0, pltpu.roll(x, cols - 1, 1))

    def last_col(x):
        return jnp.where(col_at == 0, 0.0, pltpu.roll(x, 1, 1))

    def hessian(gi, field):
        hi, lo = split(longs[gi])
        pieces = coarse_cols // 128
        stacked = [x[:, 128 * b : 128 * b + 128] for x in (hi, lo) for b in range(pieces)]
        spread_out = dot(jnp.concatenate(stacked, axis=0), spread[...])
        upper = [
            spread_out[16 * b : 16 * b + 16]
            + spread_out[16 * (pieces + b) : 16 * (pieces + b) + 16]
            for b in range(pieces)
        ]
        long_wide = jnp.concatenate(upper, axis=1)
        edges = shorts[gi, planes]
        for p in range(planes):
            center = shorts[gi, p] + jnp.where(
                row_at < 4, long_wide[4 * p + 1 : 4 * p + 2], long_wide[4 * p + 2 : 4 * p + 3]
            )
            top = (edges[2 * p : 2 * p + 1] + long_wide[4 * p : 4 * p + 1]) * low_gain
            bottom = (
                edges[2 * p + 1 : 2 * p + 2] + long_wide[4 * p + 3 : 4 * p + 4]
            ) * high_gain
            up = jnp.where(row_at == 0, top, pltpu.roll(center, 1, 0))
            down = jnp.where(row_at == rows - 1, bottom, pltpu.roll(center, rows - 1, 0))
            field[0, p] = (down - 2.0 * center + up)
            field[1, p] = (next_col(center) - 2.0 * center + last_col(center))
            slope = down - up
            field[2, p] = (next_col(slope) - last_col(slope)) * 0.25

    def advance(gi, field):
        for p in range(planes):
            k = gi * planes + p

            def distance(index):
                value = jnp.full((8, 128), slot[index], jnp.int32)
                return (value.astype(f32) + 1.0) / slot_total

            here = distance(k)
            before = jnp.where(k > 0, distance(jnp.maximum(k - 1, 0)), 0.0)
            after = jnp.where(
                k < slots - 1,
                distance(jnp.minimum(k + 1, slots - 1)),
                (slot_total + 1.0) / slot_total,
            )
            mixing = before * (after - here) / (here * (after - before))
            bending = lens_gain * (after - here) / after
            mixing = jnp.concatenate([mixing] * wide, axis=1)
            bending = jnp.concatenate([bending] * wide, axis=1)
            old = [out[e, (p - 2) % planes] for e in range(4)]
            new = [out[e, (p - 1) % planes] for e in range(4)]
            u11, u22, u12 = [field[i, p] * bending for i in range(3)]
            bent = [
                u11 * new[0] + u12 * new[2],
                u11 * new[1] + u12 * new[3],
                u12 * new[0] + u22 * new[2],
                u12 * new[1] + u22 * new[3],
            ]
            for e in range(4):
                out[e, p] = (1.0 - mixing) * old[e] + mixing * new[e] - bent[e]

    def lens(gi, carry):
        def short_wait(cb, carry):
            at = pl.ds(pl.multiple_of(cb * block, block), block)
            pltpu.make_async_remote_copy(
                src_ref=shorts.at[gi, :, :, at],
                dst_ref=shorts.at[gi, :, :, at],
                send_sem=short_send.at[gi, cb],
                recv_sem=short_recv.at[gi, cb],
                device_id={"plane": gi},
            ).wait_recv()
            return carry

        lax.fori_loop(0, blocks, short_wait, 0)
        pltpu.make_async_remote_copy(
            src_ref=longs.at[gi],
            dst_ref=longs.at[gi],
            send_sem=long_send.at[gi],
            recv_sem=long_recv.at[gi],
            device_id={"plane": gi},
        ).wait_recv()

        hessian(gi, field_now)
        advance(gi, field_now)
        return carry

    hessian(g, field_own)
    lax.fori_loop(0, g, lens, 0)
    advance(g, field_own)

    def block_sent(cb, carry):
        edge_sent(mass_copy, cb)
        edge_sent(conv_copy, cb)
        return carry

    lax.fori_loop(0, blocks, block_sent, 0)

    def coarse_sent(j, carry):
        coarse_copy(j).wait_send()
        return carry

    lax.fori_loop(1, tiles, coarse_sent, 0)

    def later_sent(to, carry):
        def short_sent(cb, inner):
            short_copy(cb, to).wait_send()
            return inner

        lax.fori_loop(0, blocks, short_sent, 0)
        long_copy(to).wait_send()
        return carry

    lax.fori_loop(g + 1, groups, later_sent, 0)


def solution(mesh):
    tiles, groups = mesh.shape["tile"], mesh.shape["plane"]

    def body(density, plane_slot, paint_weight, paint_bias, mix_weight, short_kernel):
        planes, rows, cols = density.shape
        channels = paint_weight.shape[0]
        coarse_cols = cols // 4
        blocks = cols // block
        vmem = pl.BlockSpec(memory_space=pltpu.VMEM)
        smem = pl.BlockSpec(memory_space=pltpu.SMEM)
        wide = cols + 2 * pad
        dma = pltpu.SemaphoreType.DMA
        map_shape = pltpu.VMEM((planes, rows, wide), f32)
        return pl.pallas_call(
            functools.partial(kernel, tiles, groups),
            out_shape=jax.ShapeDtypeStruct((4, planes, rows, cols), f32),
            in_specs=[vmem] + [smem] * 5,
            out_specs=vmem,
            scratch_shapes=[
                map_shape,
                map_shape,
                map_shape,
                map_shape,
                pltpu.VMEM((8 * channels, 192), bf16),
                pltpu.VMEM((16, 240), bf16),
                pltpu.VMEM((coarse_cols, coarse_cols), bf16),
                pltpu.VMEM((coarse_cols, coarse_cols), bf16),
                pltpu.VMEM((128, span), bf16),
                pltpu.VMEM((tiles, 8, coarse_cols), f32),
                pltpu.VMEM((groups, planes + 1, rows, cols), f32),
                pltpu.VMEM((groups, 16, coarse_cols), f32),
                pltpu.VMEM((8, cols), f32),
                pltpu.VMEM((3, planes, rows, cols), f32),
                pltpu.VMEM((3, planes, rows, cols), f32),
                dma((2, blocks)),
                dma((2, blocks)),
                dma((2, blocks)),
                dma((2, blocks)),
                dma((tiles,)),
                dma((tiles,)),
                dma((groups, blocks)),
                dma((groups, blocks)),
                dma((groups,)),
                dma((groups,)),
            ],
            compiler_params=pltpu.CompilerParams(
                collective_id=0, has_side_effects=True, vmem_limit_bytes=48 * 1024 * 1024
            ),
        )(density, plane_slot, paint_weight, paint_bias, mix_weight, short_kernel)

    placed = (P("plane", "tile", None), P(), P(), P(), P(), P())
    return jax.shard_map(
        body, mesh=mesh, in_specs=placed, out_specs=P(None, "plane", "tile", None), check_vma=False
    )
```

```python
import functools
import math

import jax
import jax.numpy as jnp
from jax import lax
from jax.experimental import pallas as pl
from jax.experimental.pallas import tpu as pltpu
from jax.sharding import PartitionSpec as P

lens_gain = 0.25
pad = 128
block = 512
span = 512
f32 = jnp.float32
bf16 = jnp.bfloat16


def split(x):
    hi = x.astype(bf16)
    return hi, (x - hi.astype(f32)).astype(bf16)


def iota(shape, axis):
    return lax.broadcasted_iota(jnp.int32, shape, axis)


def dot(a, b):
    return jnp.dot(a, b, preferred_element_type=f32)


def kernel(
    tiles, groups, density, slot, weight, bias, mix, short, out,
    mass_own, mass_edge, conv_own, conv_edge, paint_lhs, short_lhs, col_hi, col_lo, spread,
    gathered, shorts, longs, row_sums, field_own, field_now,
    mass_send, mass_recv, conv_send, conv_recv, coarse_send, coarse_recv,
    short_send, short_recv, long_send, long_recv, pass_send, pass_recv,
):
    planes, rows, cols = density.shape
    channels = weight.shape[0]
    slots = slot.shape[0]
    blocks = cols // block
    coarse_cols = cols // 4
    half = rows // 2
    t = lax.axis_index("tile")
    g = lax.axis_index("plane")
    has_low = t > 0
    has_high = t < tiles - 1

    def place_of(start, size):
        return pl.ds(start if isinstance(start, int) else pl.multiple_of(start, pad), size)

    def at_block(cb):
        return place_of(cb * block, block)

    def at_padded(cb):
        return place_of(cb * block + pad, block)

    def at_window(cb):
        return place_of(cb * block, block + 2 * pad)

    def shifted(x, by):
        moved = x if by == 0 else pltpu.roll(x, (-by) % (block + 2 * pad), 1)
        return moved[:, pad : pad + block]

    barrier = pltpu.get_barrier_semaphore()

    def greet_tile(j, carry):
        pl.semaphore_signal(barrier, inc=1, device_id={"tile": lax.rem(t + j, tiles)})
        return carry

    def greet_plane(j, carry):
        pl.semaphore_signal(barrier, inc=1, device_id={"plane": lax.rem(g + j, groups)})
        return carry

    lax.fori_loop(1, tiles, greet_tile, 0)
    lax.fori_loop(1, groups, greet_plane, 0)
    pl.semaphore_wait(barrier, tiles + groups - 2)

    def edge_copy(source, source_at, target, send, recv, side, cb):
        take = pl.ds(half, half) if side == 0 else pl.ds(0, half)
        give = pl.ds(0, half) if side == 0 else pl.ds(half, half)
        return pltpu.make_async_remote_copy(
            src_ref=source.at[:, take, source_at(cb)],
            dst_ref=target.at[:, give, at_padded(cb)],
            send_sem=send.at[side, cb],
            recv_sem=recv.at[side, cb],
            device_id={"tile": lax.rem(t + (1 if side == 0 else tiles - 1), tiles)},
        )

    def mass_copy(side, cb):
        return edge_copy(density, at_block, mass_edge, mass_send, mass_recv, side, cb)

    def conv_copy(side, cb):
        return edge_copy(conv_own, at_padded, conv_edge, conv_send, conv_recv, side, cb)

    def edge_start(copy, cb):
        @pl.when(has_high)
        def _():
            copy(0, cb).start()

        @pl.when(has_low)
        def _():
            copy(1, cb).start()

    def edge_wait(copy, cb):
        @pl.when(has_low)
        def _():
            copy(0, cb).wait_recv()

        @pl.when(has_high)
        def _():
            copy(1, cb).wait_recv()

    def edge_sent(copy, cb):
        @pl.when(has_high)
        def _():
            copy(0, cb).wait_send()

        @pl.when(has_low)
        def _():
            copy(1, cb).wait_send()

    def mass_start(cb, carry):
        edge_start(mass_copy, cb)
        return carry

    lax.fori_loop(0, blocks, mass_start, 0)

    for buffer in (mass_own, mass_edge, conv_own, conv_edge):
        buffer[:, :, 0:pad] = jnp.zeros((planes, rows, pad), f32)
        buffer[:, :, pad + cols :] = jnp.zeros((planes, rows, pad), f32)
    for buffer in (mass_edge, conv_edge):

        @pl.when(jnp.logical_not(has_low))
        def _():
            buffer[:, 0:half, pad : pad + cols] = jnp.zeros((planes, half, cols), f32)

        @pl.when(jnp.logical_not(has_high))
        def _():
            buffer[:, half:rows, pad : pad + cols] = jnp.zeros((planes, half, cols), f32)

    def row_of_place(place):
        return jnp.where(place < half, place - half, jnp.where(place < rows, place + half, place - rows))

    def pack(value, lane, size):
        hi = value.astype(bf16).astype(f32)
        return jnp.where(lane < 2 * size, hi, value - hi).astype(bf16)

    lane = iota((16, 192), 1)
    sub = iota((16, 192), 0)
    seg = lane & 63
    part = seg >> 4
    step = row_of_place(seg & 15) - (sub & 7)
    tap_masks = []
    for i in range(3):
        for j in range(3):
            tap_masks.append((part == j) & (step == 2 * (i - 1)))
    bias_mask = seg == 48
    first = sub < 8

    def paint_pair(c, carry):
        value = jnp.where(bias_mask, jnp.where(first, bias[2 * c], bias[2 * c + 1]), 0.0)
        for tap in range(9):
            pair = jnp.where(first, weight[2 * c, tap], weight[2 * c + 1, tap])
            value = jnp.where(tap_masks[tap], pair, value)
        paint_lhs[pl.ds(pl.multiple_of(c * 16, 16), 16), :] = pack(value, lane, 64)
        return carry

    lax.fori_loop(0, channels // 2, paint_pair, 0)
    one_row = jnp.where(iota((16, block), 0) == 0, 1.0, 0.0).astype(f32)

    lane = iota((16, 240), 1)
    sub = iota((16, 240), 0)
    seg = jnp.where(lane >= 160, lane - 160, jnp.where(lane >= 80, lane - 80, lane))
    part = seg >> 4
    step = row_of_place(seg & 15) - jnp.where(sub < 8, sub, jnp.where(sub == 8, -1, 8))
    value = jnp.zeros((16, 240), f32)
    for a in range(5):
        for b in range(5):
            value = jnp.where((part == b) & (step == a - 2) & (sub < 10), short[a, b], value)
    short_lhs[...] = pack(value, lane, 80)

    spread[...] = ((iota((128, span), 1) >> 2) == iota((128, span), 0)).astype(f32).astype(bf16)
    pool = ((iota((span, 128), 0) >> 2) == iota((span, 128), 1)).astype(f32).astype(bf16)
    col_scale = cols / 16.0

    def col_rows(i, carry):
        gap = iota((64, coarse_cols), 0) + i * 64 - iota((64, coarse_cols), 1)
        hi, lo = split(jnp.exp(-jnp.abs(gap.astype(f32)) / col_scale))
        at = pl.ds(pl.multiple_of(i * 64, 64), 64)
        col_hi[at, :] = hi
        col_lo[at, :] = lo
        return carry

    lax.fori_loop(0, coarse_cols // 64, col_rows, 0)
    mass_own[:, :, pad : pad + cols] = density[...]
    for cb in range(blocks):
        edge_wait(mass_copy, cb)

    def paint(cb):
        sums = []
        for p in range(planes):
            parts = [mass_edge[p, :, at_window(cb)], mass_own[p, :, at_window(cb)]]
            stacked = []
            for j in range(3):
                stacked += [shifted(x, 2 * (j - 1)) for x in parts]
            stacked.append(one_row)
            hi, lo = split(jnp.concatenate(stacked, axis=0))
            pre = dot(paint_lhs[...], jnp.concatenate([hi, lo, hi], axis=0))
            total = jnp.zeros((rows, block), f32)
            for c in range(channels):
                total += mix[c] * jnp.tanh(pre[rows * c : rows * c + rows])
            conv_own[p, :, at_padded(cb)] = total
            sums.append(jnp.sum(total[0:4], axis=0, keepdims=True))
            sums.append(jnp.sum(total[4:8], axis=0, keepdims=True))
        sums += [jnp.zeros((1, block), f32)] * (8 - 2 * planes)
        row_sums[:, at_block(cb)] = jnp.concatenate(sums, axis=0) * (1.0 / 16.0)

    def pool_columns():
        count = cols // span
        sums = row_sums[...]
        pieces = [sums[:, span * b : span * b + span] for b in range(count)]
        hi, lo = split(jnp.concatenate(pieces, axis=0))
        pooled = dot(jnp.concatenate([hi, lo], axis=0), pool)
        for b in range(count):
            gathered[t, :, 128 * b : 128 * b + 128] = (
                pooled[8 * b : 8 * b + 8] + pooled[8 * (count + b) : 8 * (count + b) + 8]
            )

    def short_copy(cb, to):
        return pltpu.make_async_remote_copy(
            src_ref=shorts.at[g, 0:planes, :, at_block(cb)],
            dst_ref=shorts.at[g, 0:planes, :, at_block(cb)],
            send_sem=short_send.at[to, cb],
            recv_sem=short_recv.at[g, cb],
            device_id={"plane": to},
        )

    def long_copy(to):
        return pltpu.make_async_remote_copy(
            src_ref=longs.at[g],
            dst_ref=longs.at[g],
            send_sem=long_send.at[to],
            recv_sem=long_recv.at[g],
            device_id={"plane": to},
        )

    def short_block(cb):
        edges = []
        for p in range(planes):
            parts = [conv_edge[p, :, at_window(cb)], conv_own[p, :, at_window(cb)]]
            stacked = [shifted(x, b - 2) for b in range(5) for x in parts]
            hi, lo = split(jnp.concatenate(stacked, axis=0))
            value = dot(short_lhs[...], jnp.concatenate([hi, lo, hi], axis=0))
            shorts[g, p, :, at_block(cb)] = value[0:8]
            edges.append(value[8:10])
        edges += [jnp.zeros((8 - 2 * planes, block), f32)]
        shorts[g, planes, :, at_block(cb)] = jnp.concatenate(edges, axis=0)

        def short_start(to, carry):
            short_copy(cb, to).start()
            return carry

        lax.fori_loop(g + 1, groups, short_start, 0)

    def coarse_copy(j):
        return pltpu.make_async_remote_copy(
            src_ref=gathered.at[t],
            dst_ref=gathered.at[t],
            send_sem=coarse_send.at[j],
            recv_sem=coarse_recv.at[t],
            device_id={"tile": lax.rem(t + j, tiles)},
        )

    def coarse_start(j, carry):
        coarse_copy(j).start()
        return carry

    for cb in range(blocks):
        paint(cb)
        if cb + 1 < blocks:
            edge_start(conv_copy, cb)

    pool_columns()
    lax.fori_loop(1, tiles, coarse_start, 0)
    edge_start(conv_copy, blocks - 1)
    edge_wait(conv_copy, 0)
    for cb in range(blocks):
        if cb + 1 < blocks:
            edge_wait(conv_copy, cb + 1)
        short_block(cb)

    def coarse_wait(j, carry):
        source = lax.rem(t + j, tiles)
        pltpu.make_async_remote_copy(
            src_ref=gathered.at[source],
            dst_ref=gathered.at[source],
            send_sem=coarse_send.at[j],
            recv_sem=coarse_recv.at[source],
            device_id={"tile": source},
        ).wait_recv()
        return carry

    row_scale = tiles * rows / 16.0
    long_gain = 1.0 / math.sqrt(row_scale * col_scale)
    m = iota((16, tiles * 8), 0)
    n = iota((16, tiles * 8), 1)
    gap = (2 * t - 1 + (m & 3)) - (2 * (n >> 3) + (n & 1))
    near = jnp.exp(-jnp.abs(gap.astype(f32)) / row_scale) * long_gain
    row_kernel = jnp.where((m >> 2) == ((n & 7) >> 1), near, 0.0)
    row_hi, row_lo = split(row_kernel)
    row_lhs = jnp.concatenate([row_hi, row_hi, row_lo], axis=1)
    lax.fori_loop(1, tiles, coarse_wait, 0)
    hi, lo = split(gathered[...].reshape(tiles * 8, coarse_cols))
    hi, lo = split(dot(row_lhs, jnp.concatenate([hi, lo, hi], axis=0)))
    both = dot(jnp.concatenate([hi, lo], axis=0), col_hi[...])
    longs[g] = both[0:16] + both[16:32] + dot(hi, col_lo[...])

    def long_start(to, carry):
        long_copy(to).start()
        return carry

    lax.fori_loop(g + 1, groups, long_start, 0)

    for entry in range(4):
        for p in (planes - 2, planes - 1):
            out[entry, p] = jnp.full((rows, cols), 1.0 if entry in (0, 3) else 0.0, f32)
    row_at = iota((rows, cols), 0)
    col_at = iota((rows, cols), 1)
    slot_total = 2.0 * slots
    wide = cols // 128

    def next_col(x):
        return jnp.where(col_at == cols - 1, 0.0, pltpu.roll(x, cols - 1, 1))

    def last_col(x):
        return jnp.where(col_at == 0, 0.0, pltpu.roll(x, 1, 1))

    def hessian(gi, field):
        hi, lo = split(longs[gi])
        pieces = coarse_cols // 128
        stacked = [x[:, 128 * b : 128 * b + 128] for x in (hi, lo) for b in range(pieces)]
        spread_out = dot(jnp.concatenate(stacked, axis=0), spread[...])
        upper = [
            spread_out[16 * b : 16 * b + 16]
            + spread_out[16 * (pieces + b) : 16 * (pieces + b) + 16]
            for b in range(pieces)
        ]
        long_wide = jnp.concatenate(upper, axis=1)
        edges = shorts[gi, planes]
        for p in range(planes):
            center = shorts[gi, p] + jnp.where(
                row_at < 4, long_wide[4 * p + 1 : 4 * p + 2], long_wide[4 * p + 2 : 4 * p + 3]
            )
            top = edges[2 * p : 2 * p + 1] + long_wide[4 * p : 4 * p + 1]
            top = jnp.where(has_low, top, 0.0)
            bottom = edges[2 * p + 1 : 2 * p + 2] + long_wide[4 * p + 3 : 4 * p + 4]
            bottom = jnp.where(has_high, bottom, 0.0)
            up = jnp.where(row_at == 0, top, pltpu.roll(center, 1, 0))
            down = jnp.where(row_at == rows - 1, bottom, pltpu.roll(center, rows - 1, 0))
            field[0, p] = (down - 2.0 * center + up)
            field[1, p] = (next_col(center) - 2.0 * center + last_col(center))
            slope = down - up
            field[2, p] = (next_col(slope) - last_col(slope)) * 0.25

    def advance(gi, field):
        for p in range(planes):
            k = gi * planes + p

            def distance(index):
                value = jnp.full((8, 128), slot[index], jnp.int32)
                return (value.astype(f32) + 1.0) / slot_total

            here = distance(k)
            before = jnp.where(k > 0, distance(jnp.maximum(k - 1, 0)), 0.0)
            after = jnp.where(
                k < slots - 1,
                distance(jnp.minimum(k + 1, slots - 1)),
                (slot_total + 1.0) / slot_total,
            )
            mixing = before * (after - here) / (here * (after - before))
            bending = lens_gain * (after - here) / after
            mixing = jnp.concatenate([mixing] * wide, axis=1)
            bending = jnp.concatenate([bending] * wide, axis=1)
            old = [out[e, (p - 2) % planes] for e in range(4)]
            new = [out[e, (p - 1) % planes] for e in range(4)]
            u11, u22, u12 = [field[i, p] * bending for i in range(3)]
            bent = [
                u11 * new[0] + u12 * new[2],
                u11 * new[1] + u12 * new[3],
                u12 * new[0] + u22 * new[2],
                u12 * new[1] + u22 * new[3],
            ]
            for e in range(4):
                out[e, p] = (1.0 - mixing) * old[e] + mixing * new[e] - bent[e]

    def pass_copy(side, gi, p):
        row = rows - 1 if side == 0 else 0
        return pltpu.make_async_remote_copy(
            src_ref=shorts.at[gi, p, row : row + 1, :],
            dst_ref=shorts.at[gi, planes, 2 * p + side : 2 * p + side + 1, :],
            send_sem=pass_send.at[side, gi, p],
            recv_sem=pass_recv.at[side, gi, p],
            device_id={"tile": lax.rem(t + (1 if side == 0 else tiles - 1), tiles)},
        )

    def pass_all(gi, todo):
        for p in range(planes):
            todo(lambda side, cb: pass_copy(side, cb, p), gi)

    def lens(gi, carry):
        def short_wait(cb, carry):
            at = pl.ds(pl.multiple_of(cb * block, block), block)
            pltpu.make_async_remote_copy(
                src_ref=shorts.at[gi, 0:planes, :, at],
                dst_ref=shorts.at[gi, 0:planes, :, at],
                send_sem=short_send.at[gi, cb],
                recv_sem=short_recv.at[gi, cb],
                device_id={"plane": gi},
            ).wait_recv()
            return carry

        lax.fori_loop(0, blocks, short_wait, 0)
        pass_all(gi, edge_start)
        pltpu.make_async_remote_copy(
            src_ref=longs.at[gi],
            dst_ref=longs.at[gi],
            send_sem=long_send.at[gi],
            recv_sem=long_recv.at[gi],
            device_id={"plane": gi},
        ).wait_recv()

        pass_all(gi, edge_wait)
        hessian(gi, field_now)
        advance(gi, field_now)
        return carry

    hessian(g, field_own)
    lax.fori_loop(0, g, lens, 0)
    advance(g, field_own)

    def block_sent(cb, carry):
        edge_sent(mass_copy, cb)
        edge_sent(conv_copy, cb)
        return carry

    lax.fori_loop(0, blocks, block_sent, 0)

    def passed(gi, carry):
        pass_all(gi, edge_sent)
        return carry

    lax.fori_loop(0, g, passed, 0)

    def coarse_sent(j, carry):
        coarse_copy(j).wait_send()
        return carry

    lax.fori_loop(1, tiles, coarse_sent, 0)

    def later_sent(to, carry):
        def short_sent(cb, inner):
            short_copy(cb, to).wait_send()
            return inner

        lax.fori_loop(0, blocks, short_sent, 0)
        long_copy(to).wait_send()
        return carry

    lax.fori_loop(g + 1, groups, later_sent, 0)


def solution(mesh):
    tiles, groups = mesh.shape["tile"], mesh.shape["plane"]

    def body(density, plane_slot, paint_weight, paint_bias, mix_weight, short_kernel):
        planes, rows, cols = density.shape
        channels = paint_weight.shape[0]
        coarse_cols = cols // 4
        blocks = cols // block
        vmem = pl.BlockSpec(memory_space=pltpu.VMEM)
        smem = pl.BlockSpec(memory_space=pltpu.SMEM)
        wide = cols + 2 * pad
        dma = pltpu.SemaphoreType.DMA
        map_shape = pltpu.VMEM((planes, rows, wide), f32)
        return pl.pallas_call(
            functools.partial(kernel, tiles, groups),
            out_shape=jax.ShapeDtypeStruct((4, planes, rows, cols), f32),
            in_specs=[vmem] + [smem] * 5,
            out_specs=vmem,
            scratch_shapes=[
                map_shape,
                map_shape,
                map_shape,
                map_shape,
                pltpu.VMEM((8 * channels, 192), bf16),
                pltpu.VMEM((16, 240), bf16),
                pltpu.VMEM((coarse_cols, coarse_cols), bf16),
                pltpu.VMEM((coarse_cols, coarse_cols), bf16),
                pltpu.VMEM((128, span), bf16),
                pltpu.VMEM((tiles, 8, coarse_cols), f32),
                pltpu.VMEM((groups, planes + 1, rows, cols), f32),
                pltpu.VMEM((groups, 16, coarse_cols), f32),
                pltpu.VMEM((8, cols), f32),
                pltpu.VMEM((3, planes, rows, cols), f32),
                pltpu.VMEM((3, planes, rows, cols), f32),
                dma((2, blocks)),
                dma((2, blocks)),
                dma((2, blocks)),
                dma((2, blocks)),
                dma((tiles,)),
                dma((tiles,)),
                dma((groups, blocks)),
                dma((groups, blocks)),
                dma((groups,)),
                dma((groups,)),
                dma((2, groups, planes)),
                dma((2, groups, planes)),
            ],
            compiler_params=pltpu.CompilerParams(
                collective_id=0, has_side_effects=True, vmem_limit_bytes=48 * 1024 * 1024
            ),
        )(density, plane_slot, paint_weight, paint_bias, mix_weight, short_kernel)

    placed = (P("plane", "tile", None), P(), P(), P(), P(), P())
    return jax.shard_map(
        body, mesh=mesh, in_specs=placed, out_specs=P(None, "plane", "tile", None), check_vma=False
    )
```

```python
import functools
import math

import jax
import jax.numpy as jnp
from jax import lax
from jax.experimental import pallas as pl
from jax.experimental.pallas import tpu as pltpu
from jax.sharding import PartitionSpec as P

lens_gain = 0.25
pad = 128
block = 512
span = 512
f32 = jnp.float32
bf16 = jnp.bfloat16


def split(x):
    hi = x.astype(bf16)
    return hi, (x - hi.astype(f32)).astype(bf16)


def iota(shape, axis):
    return lax.broadcasted_iota(jnp.int32, shape, axis)


def dot(a, b):
    return jnp.dot(a, b, preferred_element_type=f32)


def kernel(
    tiles, groups, density, slot, weight, bias, mix, short, out,
    mass_own, mass_edge, conv_own, conv_edge, paint_lhs, short_lhs, col_hi, col_lo, spread,
    gathered, shorts, longs, row_sums, field_own, field_now,
    mass_send, mass_recv, conv_send, conv_recv, coarse_send, coarse_recv,
    short_send, short_recv, long_send, long_recv, rim_send, rim_recv,
):
    planes, rows, cols = density.shape
    channels = weight.shape[0]
    slots = slot.shape[0]
    blocks = cols // block
    coarse_cols = cols // 4
    half = rows // 2
    t = lax.axis_index("tile")
    g = lax.axis_index("plane")
    has_low = t > 0
    has_high = t < tiles - 1

    def place_of(start, size):
        return pl.ds(start if isinstance(start, int) else pl.multiple_of(start, pad), size)

    def at_block(cb):
        return place_of(cb * block, block)

    def at_padded(cb):
        return place_of(cb * block + pad, block)

    def at_window(cb):
        return place_of(cb * block, block + 2 * pad)

    def shifted(x, by):
        moved = x if by == 0 else pltpu.roll(x, (-by) % (block + 2 * pad), 1)
        return moved[:, pad : pad + block]

    barrier = pltpu.get_barrier_semaphore()

    def greet_tile(j, carry):
        pl.semaphore_signal(barrier, inc=1, device_id={"tile": lax.rem(t + j, tiles)})
        return carry

    def greet_plane(j, carry):
        pl.semaphore_signal(barrier, inc=1, device_id={"plane": lax.rem(g + j, groups)})
        return carry

    lax.fori_loop(1, tiles, greet_tile, 0)
    lax.fori_loop(1, groups, greet_plane, 0)
    pl.semaphore_wait(barrier, tiles + groups - 2)

    def edge_copy(source, source_at, target, send, recv, side, cb):
        take = pl.ds(half, half) if side == 0 else pl.ds(0, half)
        give = pl.ds(0, half) if side == 0 else pl.ds(half, half)
        return pltpu.make_async_remote_copy(
            src_ref=source.at[:, take, source_at(cb)],
            dst_ref=target.at[:, give, at_padded(cb)],
            send_sem=send.at[side, cb],
            recv_sem=recv.at[side, cb],
            device_id={"tile": lax.rem(t + (1 if side == 0 else tiles - 1), tiles)},
        )

    def mass_copy(side, cb):
        return edge_copy(density, at_block, mass_edge, mass_send, mass_recv, side, cb)

    def conv_copy(side, cb):
        return edge_copy(conv_own, at_padded, conv_edge, conv_send, conv_recv, side, cb)

    def edge_start(copy, cb):
        @pl.when(has_high)
        def _():
            copy(0, cb).start()

        @pl.when(has_low)
        def _():
            copy(1, cb).start()

    def edge_wait(copy, cb):
        @pl.when(has_low)
        def _():
            copy(0, cb).wait_recv()

        @pl.when(has_high)
        def _():
            copy(1, cb).wait_recv()

    def edge_sent(copy, cb):
        @pl.when(has_high)
        def _():
            copy(0, cb).wait_send()

        @pl.when(has_low)
        def _():
            copy(1, cb).wait_send()

    def mass_start(cb, carry):
        edge_start(mass_copy, cb)
        return carry

    lax.fori_loop(0, blocks, mass_start, 0)

    for buffer in (mass_own, mass_edge, conv_own, conv_edge):
        buffer[:, :, 0:pad] = jnp.zeros((planes, rows, pad), f32)
        buffer[:, :, pad + cols :] = jnp.zeros((planes, rows, pad), f32)
    for buffer in (mass_edge, conv_edge):

        @pl.when(jnp.logical_not(has_low))
        def _():
            buffer[:, 0:half, pad : pad + cols] = jnp.zeros((planes, half, cols), f32)

        @pl.when(jnp.logical_not(has_high))
        def _():
            buffer[:, half:rows, pad : pad + cols] = jnp.zeros((planes, half, cols), f32)

    def row_of_place(place):
        return jnp.where(place < half, place - half, jnp.where(place < rows, place + half, place - rows))

    def pack(value, lane, size):
        hi = value.astype(bf16).astype(f32)
        return jnp.where(lane < 2 * size, hi, value - hi).astype(bf16)

    lane = iota((16, 192), 1)
    sub = iota((16, 192), 0)
    seg = lane & 63
    part = seg >> 4
    step = row_of_place(seg & 15) - (sub & 7)
    tap_masks = []
    for i in range(3):
        for j in range(3):
            tap_masks.append((part == j) & (step == 2 * (i - 1)))
    bias_mask = seg == 48
    first = sub < 8

    def paint_pair(c, carry):
        value = jnp.where(bias_mask, jnp.where(first, bias[2 * c], bias[2 * c + 1]), 0.0)
        for tap in range(9):
            pair = jnp.where(first, weight[2 * c, tap], weight[2 * c + 1, tap])
            value = jnp.where(tap_masks[tap], pair, value)
        paint_lhs[pl.ds(pl.multiple_of(c * 16, 16), 16), :] = pack(value, lane, 64)
        return carry

    lax.fori_loop(0, channels // 2, paint_pair, 0)
    one_row = jnp.where(iota((16, block), 0) == 0, 1.0, 0.0).astype(f32)

    lane = iota((16, 240), 1)
    sub = iota((16, 240), 0)
    seg = jnp.where(lane >= 160, lane - 160, jnp.where(lane >= 80, lane - 80, lane))
    part = seg >> 4
    step = row_of_place(seg & 15) - jnp.where(sub < 8, sub, jnp.where(sub == 8, -1, 8))
    value = jnp.zeros((16, 240), f32)
    for a in range(5):
        for b in range(5):
            value = jnp.where((part == b) & (step == a - 2) & (sub < 10), short[a, b], value)
    short_lhs[...] = pack(value, lane, 80)

    spread[...] = ((iota((128, span), 1) >> 2) == iota((128, span), 0)).astype(f32).astype(bf16)
    pool = ((iota((span, 128), 0) >> 2) == iota((span, 128), 1)).astype(f32).astype(bf16)
    col_scale = cols / 16.0

    def col_rows(i, carry):
        gap = iota((64, coarse_cols), 0) + i * 64 - iota((64, coarse_cols), 1)
        hi, lo = split(jnp.exp(-jnp.abs(gap.astype(f32)) / col_scale))
        at = pl.ds(pl.multiple_of(i * 64, 64), 64)
        col_hi[at, :] = hi
        col_lo[at, :] = lo
        return carry

    lax.fori_loop(0, coarse_cols // 64, col_rows, 0)
    mass_own[:, :, pad : pad + cols] = density[...]
    for cb in range(blocks):
        edge_wait(mass_copy, cb)

    def paint(cb):
        sums = []
        for p in range(planes):
            parts = [mass_edge[p, :, at_window(cb)], mass_own[p, :, at_window(cb)]]
            stacked = []
            for j in range(3):
                stacked += [shifted(x, 2 * (j - 1)) for x in parts]
            stacked.append(one_row)
            hi, lo = split(jnp.concatenate(stacked, axis=0))
            pre = dot(paint_lhs[...], jnp.concatenate([hi, lo, hi], axis=0))
            total = jnp.zeros((rows, block), f32)
            for c in range(channels):
                total += mix[c] * jnp.tanh(pre[rows * c : rows * c + rows])
            conv_own[p, :, at_padded(cb)] = total
            sums.append(jnp.sum(total[0:4], axis=0, keepdims=True))
            sums.append(jnp.sum(total[4:8], axis=0, keepdims=True))
        sums += [jnp.zeros((1, block), f32)] * (8 - 2 * planes)
        row_sums[:, at_block(cb)] = jnp.concatenate(sums, axis=0) * (1.0 / 16.0)

    def pool_columns():
        count = cols // span
        sums = row_sums[...]
        pieces = [sums[:, span * b : span * b + span] for b in range(count)]
        hi, lo = split(jnp.concatenate(pieces, axis=0))
        pooled = dot(jnp.concatenate([hi, lo], axis=0), pool)
        for b in range(count):
            gathered[t, :, 128 * b : 128 * b + 128] = (
                pooled[8 * b : 8 * b + 8] + pooled[8 * (count + b) : 8 * (count + b) + 8]
            )

    def short_copy(cb, to):
        return pltpu.make_async_remote_copy(
            src_ref=shorts.at[g, 0:planes, :, at_block(cb)],
            dst_ref=shorts.at[g, 0:planes, :, at_block(cb)],
            send_sem=short_send.at[to, cb],
            recv_sem=short_recv.at[g, cb],
            device_id={"plane": to},
        )

    def rim_copy(source, to):
        rim = shorts.at[source, planes, 0 : 2 * planes, :]
        return pltpu.make_async_remote_copy(
            src_ref=rim,
            dst_ref=rim,
            send_sem=rim_send.at[to],
            recv_sem=rim_recv.at[source],
            device_id={"plane": to},
        )

    def long_copy(to):
        return pltpu.make_async_remote_copy(
            src_ref=longs.at[g],
            dst_ref=longs.at[g],
            send_sem=long_send.at[to],
            recv_sem=long_recv.at[g],
            device_id={"plane": to},
        )

    def short_block(cb):
        edges = []
        for p in range(planes):
            parts = [conv_edge[p, :, at_window(cb)], conv_own[p, :, at_window(cb)]]
            stacked = [shifted(x, b - 2) for b in range(5) for x in parts]
            hi, lo = split(jnp.concatenate(stacked, axis=0))
            value = dot(short_lhs[...], jnp.concatenate([hi, lo, hi], axis=0))
            shorts[g, p, :, at_block(cb)] = value[0:8]
            edges.append(value[8:10])
        edges += [jnp.zeros((8 - 2 * planes, block), f32)]
        shorts[g, planes, :, at_block(cb)] = jnp.concatenate(edges, axis=0)

        def short_start(to, carry):
            short_copy(cb, to).start()
            return carry

        lax.fori_loop(g + 1, groups, short_start, 0)

    def coarse_copy(j):
        return pltpu.make_async_remote_copy(
            src_ref=gathered.at[t],
            dst_ref=gathered.at[t],
            send_sem=coarse_send.at[j],
            recv_sem=coarse_recv.at[t],
            device_id={"tile": lax.rem(t + j, tiles)},
        )

    def coarse_start(j, carry):
        coarse_copy(j).start()
        return carry

    for cb in range(blocks):
        paint(cb)
        if cb + 1 < blocks:
            edge_start(conv_copy, cb)
        if cb == 2:
            edge_wait(conv_copy, 0)
        if cb >= 2:
            edge_wait(conv_copy, cb - 1)
            short_block(cb - 2)

    pool_columns()
    lax.fori_loop(1, tiles, coarse_start, 0)
    edge_start(conv_copy, blocks - 1)
    edge_wait(conv_copy, blocks - 1)
    short_block(blocks - 2)
    short_block(blocks - 1)

    def rim_start(to, carry):
        rim_copy(g, to).start()
        return carry

    lax.fori_loop(g + 1, groups, rim_start, 0)

    def coarse_wait(j, carry):
        source = lax.rem(t + j, tiles)
        pltpu.make_async_remote_copy(
            src_ref=gathered.at[source],
            dst_ref=gathered.at[source],
            send_sem=coarse_send.at[j],
            recv_sem=coarse_recv.at[source],
            device_id={"tile": source},
        ).wait_recv()
        return carry

    row_scale = tiles * rows / 16.0
    long_gain = 1.0 / math.sqrt(row_scale * col_scale)
    m = iota((16, tiles * 8), 0)
    n = iota((16, tiles * 8), 1)
    gap = (2 * t - 1 + (m & 3)) - (2 * (n >> 3) + (n & 1))
    near = jnp.exp(-jnp.abs(gap.astype(f32)) / row_scale) * long_gain
    row_kernel = jnp.where((m >> 2) == ((n & 7) >> 1), near, 0.0)
    row_hi, row_lo = split(row_kernel)
    row_lhs = jnp.concatenate([row_hi, row_hi, row_lo], axis=1)
    lax.fori_loop(1, tiles, coarse_wait, 0)
    hi, lo = split(gathered[...].reshape(tiles * 8, coarse_cols))
    hi, lo = split(dot(row_lhs, jnp.concatenate([hi, lo, hi], axis=0)))
    both = dot(jnp.concatenate([hi, lo], axis=0), col_hi[...])
    longs[g] = both[0:16] + both[16:32] + dot(hi, col_lo[...])

    def long_start(to, carry):
        long_copy(to).start()
        return carry

    lax.fori_loop(g + 1, groups, long_start, 0)

    for entry in range(4):
        for p in (planes - 2, planes - 1):
            out[entry, p] = jnp.full((rows, cols), 1.0 if entry in (0, 3) else 0.0, f32)
    row_at = iota((rows, cols), 0)
    col_at = iota((rows, cols), 1)
    low_gain = jnp.where(t > 0, 1.0, 0.0)
    high_gain = jnp.where(t < tiles - 1, 1.0, 0.0)
    slot_total = 2.0 * slots
    wide = cols // 128

    def next_col(x):
        return jnp.where(col_at == cols - 1, 0.0, pltpu.roll(x, cols - 1, 1))

    def last_col(x):
        return jnp.where(col_at == 0, 0.0, pltpu.roll(x, 1, 1))

    def hessian(gi, field):
        hi, lo = split(longs[gi])
        pieces = coarse_cols // 128
        stacked = [x[:, 128 * b : 128 * b + 128] for x in (hi, lo) for b in range(pieces)]
        spread_out = dot(jnp.concatenate(stacked, axis=0), spread[...])
        upper = [
            spread_out[16 * b : 16 * b + 16]
            + spread_out[16 * (pieces + b) : 16 * (pieces + b) + 16]
            for b in range(pieces)
        ]
        long_wide = jnp.concatenate(upper, axis=1)
        edges = shorts[gi, planes]
        for p in range(planes):
            center = shorts[gi, p] + jnp.where(
                row_at < 4, long_wide[4 * p + 1 : 4 * p + 2], long_wide[4 * p + 2 : 4 * p + 3]
            )
            top = (edges[2 * p : 2 * p + 1] + long_wide[4 * p : 4 * p + 1]) * low_gain
            bottom = (
                edges[2 * p + 1 : 2 * p + 2] + long_wide[4 * p + 3 : 4 * p + 4]
            ) * high_gain
            up = jnp.where(row_at == 0, top, pltpu.roll(center, 1, 0))
            down = jnp.where(row_at == rows - 1, bottom, pltpu.roll(center, rows - 1, 0))
            field[0, p] = (down - 2.0 * center + up)
            field[1, p] = (next_col(center) - 2.0 * center + last_col(center))
            slope = down - up
            field[2, p] = (next_col(slope) - last_col(slope)) * 0.25

    def advance(gi, field):
        for p in range(planes):
            k = gi * planes + p

            def distance(index):
                value = jnp.full((8, 128), slot[index], jnp.int32)
                return (value.astype(f32) + 1.0) / slot_total

            here = distance(k)
            before = jnp.where(k > 0, distance(jnp.maximum(k - 1, 0)), 0.0)
            after = jnp.where(
                k < slots - 1,
                distance(jnp.minimum(k + 1, slots - 1)),
                (slot_total + 1.0) / slot_total,
            )
            mixing = before * (after - here) / (here * (after - before))
            bending = lens_gain * (after - here) / after
            mixing = jnp.concatenate([mixing] * wide, axis=1)
            bending = jnp.concatenate([bending] * wide, axis=1)
            old = [out[e, (p - 2) % planes] for e in range(4)]
            new = [out[e, (p - 1) % planes] for e in range(4)]
            u11, u22, u12 = [field[i, p] * bending for i in range(3)]
            bent = [
                u11 * new[0] + u12 * new[2],
                u11 * new[1] + u12 * new[3],
                u12 * new[0] + u22 * new[2],
                u12 * new[1] + u22 * new[3],
            ]
            for e in range(4):
                out[e, p] = (1.0 - mixing) * old[e] + mixing * new[e] - bent[e]

    def lens(gi, carry):
        def short_wait(cb, carry):
            at = pl.ds(pl.multiple_of(cb * block, block), block)
            pltpu.make_async_remote_copy(
                src_ref=shorts.at[gi, 0:planes, :, at],
                dst_ref=shorts.at[gi, 0:planes, :, at],
                send_sem=short_send.at[gi, cb],
                recv_sem=short_recv.at[gi, cb],
                device_id={"plane": gi},
            ).wait_recv()
            return carry

        lax.fori_loop(0, blocks, short_wait, 0)
        pltpu.make_async_remote_copy(
            src_ref=longs.at[gi],
            dst_ref=longs.at[gi],
            send_sem=long_send.at[gi],
            recv_sem=long_recv.at[gi],
            device_id={"plane": gi},
        ).wait_recv()

        rim_copy(gi, gi).wait_recv()
        hessian(gi, field_now)
        advance(gi, field_now)
        return carry

    hessian(g, field_own)
    lax.fori_loop(0, g, lens, 0)
    advance(g, field_own)

    def block_sent(cb, carry):
        edge_sent(mass_copy, cb)
        edge_sent(conv_copy, cb)
        return carry

    lax.fori_loop(0, blocks, block_sent, 0)

    def coarse_sent(j, carry):
        coarse_copy(j).wait_send()
        return carry

    lax.fori_loop(1, tiles, coarse_sent, 0)

    def later_sent(to, carry):
        def short_sent(cb, inner):
            short_copy(cb, to).wait_send()
            return inner

        lax.fori_loop(0, blocks, short_sent, 0)
        long_copy(to).wait_send()
        rim_copy(g, to).wait_send()
        return carry

    lax.fori_loop(g + 1, groups, later_sent, 0)


def solution(mesh):
    tiles, groups = mesh.shape["tile"], mesh.shape["plane"]

    def body(density, plane_slot, paint_weight, paint_bias, mix_weight, short_kernel):
        planes, rows, cols = density.shape
        channels = paint_weight.shape[0]
        coarse_cols = cols // 4
        blocks = cols // block
        vmem = pl.BlockSpec(memory_space=pltpu.VMEM)
        smem = pl.BlockSpec(memory_space=pltpu.SMEM)
        wide = cols + 2 * pad
        dma = pltpu.SemaphoreType.DMA
        map_shape = pltpu.VMEM((planes, rows, wide), f32)
        return pl.pallas_call(
            functools.partial(kernel, tiles, groups),
            out_shape=jax.ShapeDtypeStruct((4, planes, rows, cols), f32),
            in_specs=[vmem] + [smem] * 5,
            out_specs=vmem,
            scratch_shapes=[
                map_shape,
                map_shape,
                map_shape,
                map_shape,
                pltpu.VMEM((8 * channels, 192), bf16),
                pltpu.VMEM((16, 240), bf16),
                pltpu.VMEM((coarse_cols, coarse_cols), bf16),
                pltpu.VMEM((coarse_cols, coarse_cols), bf16),
                pltpu.VMEM((128, span), bf16),
                pltpu.VMEM((tiles, 8, coarse_cols), f32),
                pltpu.VMEM((groups, planes + 1, rows, cols), f32),
                pltpu.VMEM((groups, 16, coarse_cols), f32),
                pltpu.VMEM((8, cols), f32),
                pltpu.VMEM((3, planes, rows, cols), f32),
                pltpu.VMEM((3, planes, rows, cols), f32),
                dma((2, blocks)),
                dma((2, blocks)),
                dma((2, blocks)),
                dma((2, blocks)),
                dma((tiles,)),
                dma((tiles,)),
                dma((groups, blocks)),
                dma((groups, blocks)),
                dma((groups,)),
                dma((groups,)),
                dma((groups,)),
                dma((groups,)),
            ],
            compiler_params=pltpu.CompilerParams(
                collective_id=0, has_side_effects=True, vmem_limit_bytes=48 * 1024 * 1024
            ),
        )(density, plane_slot, paint_weight, paint_bias, mix_weight, short_kernel)

    placed = (P("plane", "tile", None), P(), P(), P(), P(), P())
    return jax.shard_map(
        body, mesh=mesh, in_specs=placed, out_specs=P(None, "plane", "tile", None), check_vma=False
    )
```

```python
import functools
import math

import jax
import jax.numpy as jnp
from jax import lax
from jax.experimental import pallas as pl
from jax.experimental.pallas import tpu as pltpu
from jax.sharding import PartitionSpec as P

lens_gain = 0.25
pad = 128
block = 512
span = 512
f32 = jnp.float32
bf16 = jnp.bfloat16


def split(x):
    hi = x.astype(bf16)
    return hi, (x - hi.astype(f32)).astype(bf16)


def iota(shape, axis):
    return lax.broadcasted_iota(jnp.int32, shape, axis)


def dot(a, b):
    return jnp.dot(a, b, preferred_element_type=f32)


def kernel(
    tiles, groups, density, slot, weight, bias, mix, short, out,
    mass_own, mass_edge, conv_own, conv_edge, paint_lhs, short_lhs, col_hi, col_lo, spread,
    gathered, shorts, longs, row_sums, field_own, field_now,
    mass_send, mass_recv, conv_send, conv_recv, coarse_send, coarse_recv,
    short_send, short_recv, long_send, long_recv,
):
    planes, rows, cols = density.shape
    channels = weight.shape[0]
    slots = slot.shape[0]
    blocks = cols // block
    coarse_cols = cols // 4
    half = rows // 2
    t = lax.axis_index("tile")
    g = lax.axis_index("plane")
    has_low = t > 0
    has_high = t < tiles - 1

    def at_block(cb):
        return pl.ds(pl.multiple_of(cb * block, block), block)

    def at_padded(cb):
        return pl.ds(pl.multiple_of(cb * block + pad, pad), block)

    def at_window(cb):
        return pl.ds(pl.multiple_of(cb * block, block), block + 2 * pad)

    def shifted(x, by):
        moved = x if by == 0 else pltpu.roll(x, (-by) % (block + 2 * pad), 1)
        return moved[:, pad : pad + block]

    barrier = pltpu.get_barrier_semaphore()

    def greet_tile(j, carry):
        pl.semaphore_signal(barrier, inc=1, device_id={"tile": lax.rem(t + j, tiles)})
        return carry

    def greet_plane(j, carry):
        pl.semaphore_signal(barrier, inc=1, device_id={"plane": lax.rem(g + j, groups)})
        return carry

    lax.fori_loop(1, tiles, greet_tile, 0)
    lax.fori_loop(1, groups, greet_plane, 0)
    pl.semaphore_wait(barrier, tiles + groups - 2)

    def edge_copy(source, source_at, target, send, recv, side, cb):
        take = pl.ds(half, half) if side == 0 else pl.ds(0, half)
        give = pl.ds(0, half) if side == 0 else pl.ds(half, half)
        return pltpu.make_async_remote_copy(
            src_ref=source.at[:, take, source_at(cb)],
            dst_ref=target.at[:, give, at_padded(cb)],
            send_sem=send.at[side, cb],
            recv_sem=recv.at[side, cb],
            device_id={"tile": lax.rem(t + (1 if side == 0 else tiles - 1), tiles)},
        )

    def mass_copy(side, cb):
        return edge_copy(density, at_block, mass_edge, mass_send, mass_recv, side, cb)

    def conv_copy(side, cb):
        return edge_copy(conv_own, at_padded, conv_edge, conv_send, conv_recv, side, cb)

    def edge_start(copy, cb):
        @pl.when(has_high)
        def _():
            copy(0, cb).start()

        @pl.when(has_low)
        def _():
            copy(1, cb).start()

    def edge_wait(copy, cb):
        @pl.when(has_low)
        def _():
            copy(0, cb).wait_recv()

        @pl.when(has_high)
        def _():
            copy(1, cb).wait_recv()

    def edge_sent(copy, cb):
        @pl.when(has_high)
        def _():
            copy(0, cb).wait_send()

        @pl.when(has_low)
        def _():
            copy(1, cb).wait_send()

    def mass_start(cb, carry):
        edge_start(mass_copy, cb)
        return carry

    lax.fori_loop(0, blocks, mass_start, 0)

    for buffer in (mass_own, mass_edge, conv_own, conv_edge):
        buffer[:, :, 0:pad] = jnp.zeros((planes, rows, pad), f32)
        buffer[:, :, pad + cols :] = jnp.zeros((planes, rows, pad), f32)
    for buffer in (mass_edge, conv_edge):

        @pl.when(jnp.logical_not(has_low))
        def _():
            buffer[:, 0:half, pad : pad + cols] = jnp.zeros((planes, half, cols), f32)

        @pl.when(jnp.logical_not(has_high))
        def _():
            buffer[:, half:rows, pad : pad + cols] = jnp.zeros((planes, half, cols), f32)

    def row_of_place(place):
        return jnp.where(place < half, place - half, jnp.where(place < rows, place + half, place - rows))

    def pack(value, lane, size):
        hi = value.astype(bf16).astype(f32)
        return jnp.where(lane < 2 * size, hi, value - hi).astype(bf16)

    lane = iota((16, 192), 1)
    sub = iota((16, 192), 0)
    seg = lane & 63
    part = seg >> 4
    step = row_of_place(seg & 15) - (sub & 7)
    tap_masks = []
    for i in range(3):
        for j in range(3):
            tap_masks.append((part == j) & (step == 2 * (i - 1)))
    bias_mask = seg == 48
    first = sub < 8

    def paint_pair(c, carry):
        value = jnp.where(bias_mask, jnp.where(first, bias[2 * c], bias[2 * c + 1]), 0.0)
        for tap in range(9):
            pair = jnp.where(first, weight[2 * c, tap], weight[2 * c + 1, tap])
            value = jnp.where(tap_masks[tap], pair, value)
        paint_lhs[pl.ds(pl.multiple_of(c * 16, 16), 16), :] = pack(value, lane, 64)
        return carry

    lax.fori_loop(0, channels // 2, paint_pair, 0)
    one_row = jnp.where(iota((16, block), 0) == 0, 1.0, 0.0).astype(f32)

    lane = iota((16, 240), 1)
    sub = iota((16, 240), 0)
    seg = jnp.where(lane >= 160, lane - 160, jnp.where(lane >= 80, lane - 80, lane))
    part = seg >> 4
    step = row_of_place(seg & 15) - jnp.where(sub < 8, sub, jnp.where(sub == 8, -1, 8))
    value = jnp.zeros((16, 240), f32)
    for a in range(5):
        for b in range(5):
            value = jnp.where((part == b) & (step == a - 2) & (sub < 10), short[a, b], value)
    short_lhs[...] = pack(value, lane, 80)

    spread[...] = ((iota((128, span), 1) >> 2) == iota((128, span), 0)).astype(f32).astype(bf16)
    pool = ((iota((span, 128), 0) >> 2) == iota((span, 128), 1)).astype(f32).astype(bf16)
    col_scale = cols / 16.0

    def col_rows(i, carry):
        gap = iota((64, coarse_cols), 0) + i * 64 - iota((64, coarse_cols), 1)
        hi, lo = split(jnp.exp(-jnp.abs(gap.astype(f32)) / col_scale))
        at = pl.ds(pl.multiple_of(i * 64, 64), 64)
        col_hi[at, :] = hi
        col_lo[at, :] = lo
        return carry

    lax.fori_loop(0, coarse_cols // 64, col_rows, 0)
    mass_own[:, :, pad : pad + cols] = density[...]
    edge_wait(mass_copy, 0)

    def paint(cb):
        sums = []
        for p in range(planes):
            parts = [mass_edge[p, :, at_window(cb)], mass_own[p, :, at_window(cb)]]
            stacked = []
            for j in range(3):
                stacked += [shifted(x, 2 * (j - 1)) for x in parts]
            stacked.append(one_row)
            hi, lo = split(jnp.concatenate(stacked, axis=0))
            pre = dot(paint_lhs[...], jnp.concatenate([hi, lo, hi], axis=0))
            total = jnp.zeros((rows, block), f32)
            for c in range(channels):
                total += mix[c] * jnp.tanh(pre[rows * c : rows * c + rows])
            conv_own[p, :, at_padded(cb)] = total
            sums.append(jnp.sum(total[0:4], axis=0, keepdims=True))
            sums.append(jnp.sum(total[4:8], axis=0, keepdims=True))
        sums += [jnp.zeros((1, block), f32)] * (8 - 2 * planes)
        row_sums[:, at_block(cb)] = jnp.concatenate(sums, axis=0) * (1.0 / 16.0)

    def pool_columns():
        count = cols // span
        sums = row_sums[...]
        pieces = [sums[:, span * b : span * b + span] for b in range(count)]
        hi, lo = split(jnp.concatenate(pieces, axis=0))
        pooled = dot(jnp.concatenate([hi, lo], axis=0), pool)
        for b in range(count):
            gathered[t, :, 128 * b : 128 * b + 128] = (
                pooled[8 * b : 8 * b + 8] + pooled[8 * (count + b) : 8 * (count + b) + 8]
            )

    def short_copy(cb, to):
        return pltpu.make_async_remote_copy(
            src_ref=shorts.at[g, :, :, at_block(cb)],
            dst_ref=shorts.at[g, :, :, at_block(cb)],
            send_sem=short_send.at[to, cb],
            recv_sem=short_recv.at[g, cb],
            device_id={"plane": to},
        )

    def long_copy(to):
        return pltpu.make_async_remote_copy(
            src_ref=longs.at[g],
            dst_ref=longs.at[g],
            send_sem=long_send.at[to],
            recv_sem=long_recv.at[g],
            device_id={"plane": to},
        )

    def short_block(cb):
        edges = []
        for p in range(planes):
            parts = [conv_edge[p, :, at_window(cb)], conv_own[p, :, at_window(cb)]]
            stacked = [shifted(x, b - 2) for b in range(5) for x in parts]
            hi, lo = split(jnp.concatenate(stacked, axis=0))
            value = dot(short_lhs[...], jnp.concatenate([hi, lo, hi], axis=0))
            shorts[g, p, :, at_block(cb)] = value[0:8]
            edges.append(value[8:10])
        edges += [jnp.zeros((8 - 2 * planes, block), f32)]
        shorts[g, planes, :, at_block(cb)] = jnp.concatenate(edges, axis=0)

        def short_start(to, carry):
            short_copy(cb, to).start()
            return carry

        lax.fori_loop(g + 1, groups, short_start, 0)

    def coarse_copy(j):
        return pltpu.make_async_remote_copy(
            src_ref=gathered.at[t],
            dst_ref=gathered.at[t],
            send_sem=coarse_send.at[j],
            recv_sem=coarse_recv.at[t],
            device_id={"tile": lax.rem(t + j, tiles)},
        )

    def coarse_start(j, carry):
        coarse_copy(j).start()
        return carry

    def paint_step(cb, carry):
        @pl.when(cb + 1 < blocks)
        def _():
            edge_wait(mass_copy, cb + 1)

        paint(cb)

        @pl.when(cb + 1 < blocks)
        def _():
            edge_start(conv_copy, cb)

        @pl.when(cb == 2)
        def _():
            edge_wait(conv_copy, 0)

        @pl.when(cb > 1)
        def _():
            edge_wait(conv_copy, cb - 1)
            short_block(cb - 2)

        return carry

    lax.fori_loop(0, blocks, paint_step, 0)
    pool_columns()
    lax.fori_loop(1, tiles, coarse_start, 0)
    edge_start(conv_copy, blocks - 1)
    short_rest = max(blocks - 2, 0)

    def short_step(cb, carry):
        @pl.when(cb + 1 < blocks)
        def _():
            edge_wait(conv_copy, cb + 1)

        short_block(cb)
        return carry

    lax.fori_loop(short_rest, blocks, short_step, 0)

    def coarse_wait(j, carry):
        source = lax.rem(t + j, tiles)
        pltpu.make_async_remote_copy(
            src_ref=gathered.at[source],
            dst_ref=gathered.at[source],
            send_sem=coarse_send.at[j],
            recv_sem=coarse_recv.at[source],
            device_id={"tile": source},
        ).wait_recv()
        return carry

    row_scale = tiles * rows / 16.0
    long_gain = 1.0 / math.sqrt(row_scale * col_scale)
    m = iota((16, tiles * 8), 0)
    n = iota((16, tiles * 8), 1)
    gap = (2 * t - 1 + (m & 3)) - (2 * (n >> 3) + (n & 1))
    near = jnp.exp(-jnp.abs(gap.astype(f32)) / row_scale) * long_gain
    row_kernel = jnp.where((m >> 2) == ((n & 7) >> 1), near, 0.0)
    row_hi, row_lo = split(row_kernel)
    row_lhs = jnp.concatenate([row_hi, row_hi, row_lo], axis=1)
    lax.fori_loop(1, tiles, coarse_wait, 0)
    hi, lo = split(gathered[...].reshape(tiles * 8, coarse_cols))
    hi, lo = split(dot(row_lhs, jnp.concatenate([hi, lo, hi], axis=0)))
    both = dot(jnp.concatenate([hi, lo], axis=0), col_hi[...])
    longs[g] = both[0:16] + both[16:32] + dot(hi, col_lo[...])

    def long_start(to, carry):
        long_copy(to).start()
        return carry

    lax.fori_loop(g + 1, groups, long_start, 0)

    for entry in range(4):
        for p in (planes - 2, planes - 1):
            out[entry, p] = jnp.full((rows, cols), 1.0 if entry in (0, 3) else 0.0, f32)
    row_at = iota((rows, cols), 0)
    col_at = iota((rows, cols), 1)
    low_gain = jnp.where(t > 0, 1.0, 0.0)
    high_gain = jnp.where(t < tiles - 1, 1.0, 0.0)
    slot_total = 2.0 * slots
    wide = cols // 128

    def next_col(x):
        return jnp.where(col_at == cols - 1, 0.0, pltpu.roll(x, cols - 1, 1))

    def last_col(x):
        return jnp.where(col_at == 0, 0.0, pltpu.roll(x, 1, 1))

    def hessian(gi, field):
        hi, lo = split(longs[gi])
        pieces = coarse_cols // 128
        stacked = [x[:, 128 * b : 128 * b + 128] for x in (hi, lo) for b in range(pieces)]
        spread_out = dot(jnp.concatenate(stacked, axis=0), spread[...])
        upper = [
            spread_out[16 * b : 16 * b + 16]
            + spread_out[16 * (pieces + b) : 16 * (pieces + b) + 16]
            for b in range(pieces)
        ]
        long_wide = jnp.concatenate(upper, axis=1)
        edges = shorts[gi, planes]
        for p in range(planes):
            center = shorts[gi, p] + jnp.where(
                row_at < 4, long_wide[4 * p + 1 : 4 * p + 2], long_wide[4 * p + 2 : 4 * p + 3]
            )
            top = (edges[2 * p : 2 * p + 1] + long_wide[4 * p : 4 * p + 1]) * low_gain
            bottom = (
                edges[2 * p + 1 : 2 * p + 2] + long_wide[4 * p + 3 : 4 * p + 4]
            ) * high_gain
            up = jnp.where(row_at == 0, top, pltpu.roll(center, 1, 0))
            down = jnp.where(row_at == rows - 1, bottom, pltpu.roll(center, rows - 1, 0))
            field[0, p] = (down - 2.0 * center + up)
            field[1, p] = (next_col(center) - 2.0 * center + last_col(center))
            slope = down - up
            field[2, p] = (next_col(slope) - last_col(slope)) * 0.25

    def advance(gi, field):
        for p in range(planes):
            k = gi * planes + p

            def distance(index):
                value = jnp.full((8, 128), slot[index], jnp.int32)
                return (value.astype(f32) + 1.0) / slot_total

            here = distance(k)
            before = jnp.where(k > 0, distance(jnp.maximum(k - 1, 0)), 0.0)
            after = jnp.where(
                k < slots - 1,
                distance(jnp.minimum(k + 1, slots - 1)),
                (slot_total + 1.0) / slot_total,
            )
            mixing = before * (after - here) / (here * (after - before))
            bending = lens_gain * (after - here) / after
            mixing = jnp.concatenate([mixing] * wide, axis=1)
            bending = jnp.concatenate([bending] * wide, axis=1)
            old = [out[e, (p - 2) % planes] for e in range(4)]
            new = [out[e, (p - 1) % planes] for e in range(4)]
            u11, u22, u12 = [field[i, p] * bending for i in range(3)]
            bent = [
                u11 * new[0] + u12 * new[2],
                u11 * new[1] + u12 * new[3],
                u12 * new[0] + u22 * new[2],
                u12 * new[1] + u22 * new[3],
            ]
            for e in range(4):
                out[e, p] = (1.0 - mixing) * old[e] + mixing * new[e] - bent[e]

    def lens(gi, carry):
        def short_wait(cb, carry):
            at = pl.ds(pl.multiple_of(cb * block, block), block)
            pltpu.make_async_remote_copy(
                src_ref=shorts.at[gi, :, :, at],
                dst_ref=shorts.at[gi, :, :, at],
                send_sem=short_send.at[gi, cb],
                recv_sem=short_recv.at[gi, cb],
                device_id={"plane": gi},
            ).wait_recv()
            return carry

        lax.fori_loop(0, blocks, short_wait, 0)
        pltpu.make_async_remote_copy(
            src_ref=longs.at[gi],
            dst_ref=longs.at[gi],
            send_sem=long_send.at[gi],
            recv_sem=long_recv.at[gi],
            device_id={"plane": gi},
        ).wait_recv()

        hessian(gi, field_now)
        advance(gi, field_now)
        return carry

    hessian(g, field_own)
    lax.fori_loop(0, g, lens, 0)
    advance(g, field_own)

    def block_sent(cb, carry):
        edge_sent(mass_copy, cb)
        edge_sent(conv_copy, cb)
        return carry

    lax.fori_loop(0, blocks, block_sent, 0)

    def coarse_sent(j, carry):
        coarse_copy(j).wait_send()
        return carry

    lax.fori_loop(1, tiles, coarse_sent, 0)

    def later_sent(to, carry):
        def short_sent(cb, inner):
            short_copy(cb, to).wait_send()
            return inner

        lax.fori_loop(0, blocks, short_sent, 0)
        long_copy(to).wait_send()
        return carry

    lax.fori_loop(g + 1, groups, later_sent, 0)


def solution(mesh):
    tiles, groups = mesh.shape["tile"], mesh.shape["plane"]

    def body(density, plane_slot, paint_weight, paint_bias, mix_weight, short_kernel):
        planes, rows, cols = density.shape
        channels = paint_weight.shape[0]
        coarse_cols = cols // 4
        blocks = cols // block
        vmem = pl.BlockSpec(memory_space=pltpu.VMEM)
        smem = pl.BlockSpec(memory_space=pltpu.SMEM)
        wide = cols + 2 * pad
        dma = pltpu.SemaphoreType.DMA
        map_shape = pltpu.VMEM((planes, rows, wide), f32)
        return pl.pallas_call(
            functools.partial(kernel, tiles, groups),
            out_shape=jax.ShapeDtypeStruct((4, planes, rows, cols), f32),
            in_specs=[vmem] + [smem] * 5,
            out_specs=vmem,
            scratch_shapes=[
                map_shape,
                map_shape,
                map_shape,
                map_shape,
                pltpu.VMEM((8 * channels, 192), bf16),
                pltpu.VMEM((16, 240), bf16),
                pltpu.VMEM((coarse_cols, coarse_cols), bf16),
                pltpu.VMEM((coarse_cols, coarse_cols), bf16),
                pltpu.VMEM((128, span), bf16),
                pltpu.VMEM((tiles, 8, coarse_cols), f32),
                pltpu.VMEM((groups, planes + 1, rows, cols), f32),
                pltpu.VMEM((groups, 16, coarse_cols), f32),
                pltpu.VMEM((8, cols), f32),
                pltpu.VMEM((3, planes, rows, cols), f32),
                pltpu.VMEM((3, planes, rows, cols), f32),
                dma((2, blocks)),
                dma((2, blocks)),
                dma((2, blocks)),
                dma((2, blocks)),
                dma((tiles,)),
                dma((tiles,)),
                dma((groups, blocks)),
                dma((groups, blocks)),
                dma((groups,)),
                dma((groups,)),
            ],
            compiler_params=pltpu.CompilerParams(
                collective_id=0, has_side_effects=True, vmem_limit_bytes=48 * 1024 * 1024
            ),
        )(density, plane_slot, paint_weight, paint_bias, mix_weight, short_kernel)

    placed = (P("plane", "tile", None), P(), P(), P(), P(), P())
    return jax.shard_map(
        body, mesh=mesh, in_specs=placed, out_specs=P(None, "plane", "tile", None), check_vma=False
    )
```
